32 devices in a mesh: seq: 8 (over y, x, core), tp: 4 (over z).
Axes of the slice: x: 2, y: 2, z: 4, core: 2. Of those that a mesh axis runs over, the one named last changes fastest.
Arguments:
- vis_feat: bfloat16 [128, 12800], P('seq', 'tp'), may hold values from -256 to 256
- ln_gain: float32 [12800], P('tp'), may hold values from 0.25 to 1.75
- proj_weight: bfloat16 [12800, 8192], P('tp', 'seq'), may hold values from -0.0546875 to 0.0546875
- text_embed: bfloat16 [2048, 8192], P('seq'), may hold values from -128 to 128
- rms_gain: float32 [8192], replicated, may hold values from 0.25 to 1.75
- wq: bfloat16 [8192, 4096], P('seq', 'tp'), may hold values from -1 to 1
- wk: bfloat16 [8192, 1024], P('seq', 'tp'), may hold values from -1 to 1
- wv: bfloat16 [8192, 1024], P('seq', 'tp'), may hold values from -0.0625 to 0.0625
- doc_ids: int32 [2048], P('seq'), may hold values from 0 to 15, as said below
- vis_slot: int32 [2048], P('seq'), may hold values from -1 to 31, as said below
- slot_token: int32 [256], replicated, may hold values from -1 to 127, as said below
- token_slot: int32 [128], replicated, may hold values from 0 to 255, as said below
- cotangent: bfloat16 [2048, 4096], P('seq', 'tp'), may hold values from -6 to 6
Outputs:
- context: bfloat16 [2048, 4096], P('seq', 'tp')
- vis_grad: bfloat16 [128, 12800], P('seq', 'tp')
The draws below stay inside these ranges and needn't reach their ends.
Inputs may be any that keep to these rules, and one draw needn't show every extreme that they name: `doc_ids`: document numbers never fall along the positions and rise by one at each new document; each document has 1 to 256 positions, and one has exactly 256. `vis_slot`: in each block of 256 positions the image positions form one run that ends at the block's last position, numbered 0, 1, 2 ... in order; a block has 0 to 32 of them, 128 in all, and some block has exactly 32. `slot_token`: entry b * 32 + j names the visual token at image position j of block b, or -1 where block b has fewer image positions; each visual token is named once. `token_slot`: for each visual token, the index of the entry of slot_token that names it.
All inputs are finite; a program needn't handle non-finite values.
Results may differ from the reference program's by a relative error of at most 0.025.
Values may be sent and summed in bfloat16 or wider, within the bound.
A program may use at most 128 MiB of HBM per device.

```python
import math
import jax
import jax.numpy as jnp
from jax import lax

VF = 12800
D = 8192
HEAD = 128
KV = 8
HEADS = 32
TOK_DEV = 256
VIS_DEV = 16
CAPD = 32
GROUP = 4
TOKENS = 2048
VIS = 128
N_SEQ = 8


def routing_tables(key):
    groups = TOKENS // TOK_DEV
    pairs = groups // 2
    subkeys = jax.random.split(jax.random.fold_in(key, 501), 5)
    shifts = jax.random.randint(subkeys[0], (pairs,), 1 - VIS_DEV, VIS_DEV + 1)
    chosen = jax.random.randint(subkeys[1], (), 0, pairs)
    flip = jax.random.randint(subkeys[2], (), 0, 2) * 2 - 1
    flip = jnp.where(chosen == pairs - 1, 1, flip)
    shifts = jnp.where(jnp.arange(pairs) == chosen, flip * VIS_DEV, shifts)
    counts = jnp.stack([VIS_DEV + shifts, VIS_DEV - shifts], axis=1).reshape(groups)
    offsets = TOK_DEV - counts
    firsts = jnp.cumsum(counts) - counts
    order = jax.random.permutation(subkeys[4], VIS)
    lanes = jnp.arange(CAPD)
    live = lanes[None, :] < counts[:, None]
    picked = order[jnp.clip(firsts[:, None] + lanes[None, :], 0, VIS - 1)]
    slot_token = jnp.where(live, picked, -1).reshape(groups * CAPD)
    local = jnp.arange(TOK_DEV)[None, :] - offsets[:, None]
    vis_slot = jnp.where((local >= 0) & (local < counts[:, None]), local, -1).reshape(TOKENS)
    slot_ids = jnp.arange(groups * CAPD)
    target = jnp.where(live.reshape(groups * CAPD), picked.reshape(groups * CAPD), VIS)
    token_slot = jnp.zeros((VIS,), jnp.int32).at[target].set(slot_ids, mode='drop')
    return (slot_token.astype(jnp.int32), vis_slot.astype(jnp.int32), token_slot.astype(jnp.int32))


def draw_slot_token(key, part):
    return routing_tables(key)[0]


def draw_vis_slot(key, part):
    return routing_tables(key)[1]


def draw_token_slot(key, part):
    return routing_tables(key)[2]


def draw_doc_ids(key, part):
    groups = TOKENS // TOK_DEV
    quarter = TOK_DEV // 4
    half = TOK_DEV // 2
    subkeys = jax.random.split(jax.random.fold_in(key, 801), 3)
    index = jnp.arange(groups)
    starts = jax.random.randint(subkeys[0], (groups,), quarter, half + 1)
    gaps = jax.random.randint(subkeys[1], (groups,), 0, quarter)
    chosen = jax.random.randint(subkeys[2], (), 0, groups - 1)
    starts = jnp.where(index == chosen, quarter, starts)
    starts = jnp.where(index == chosen + 1, half, starts)
    gaps = jnp.where(starts == half, jnp.maximum(gaps, 1), gaps)
    gaps = jnp.where(index == chosen, 0, gaps)
    firsts = index * TOK_DEV
    first_cuts = (firsts + starts)[1:]
    second_cuts = firsts + half + gaps
    marks = jnp.zeros((TOKENS,), jnp.int32).at[first_cuts].set(1).at[second_cuts].set(1)
    return jnp.cumsum(marks).astype(jnp.int32)


def draw_vis_feat(key, part):
    subkeys = jax.random.split(jax.random.fold_in(key, 601), 3)
    rows = jnp.exp(jax.random.uniform(subkeys[1], (VIS, 1), minval=0.0, maxval=math.log(10.0)))
    ramp = jnp.exp(math.log(3.0) * jnp.arange(VF).astype(jnp.float32) / VF)
    rough = jnp.exp(jax.random.uniform(subkeys[2], (VF,), minval=-0.35, maxval=0.35))
    base = jnp.clip(jax.random.normal(subkeys[0], (VIS, VF)), -6.0, 6.0)
    return (base * rows * (ramp * rough)[None, :]).astype(jnp.bfloat16)


def draw_text_embed(key, part):
    subkeys = jax.random.split(jax.random.fold_in(key, 703), 2)
    rows = jnp.exp(jax.random.uniform(subkeys[1], (TOKENS, 1), minval=0.0, maxval=math.log(10.0)))
    base = jnp.clip(jax.random.normal(subkeys[0], (TOKENS, D)), -6.0, 6.0)
    return (base * rows).astype(jnp.bfloat16)


def draw_wq(key, part):
    base = jnp.clip(jax.random.normal(jax.random.fold_in(key, 704), (D, HEADS * HEAD)), -6.0, 6.0) / math.sqrt(D)
    return base.astype(jnp.bfloat16)


def draw_wk(key, part):
    base = jnp.clip(jax.random.normal(jax.random.fold_in(key, 705), (D, KV * HEAD)), -6.0, 6.0) / math.sqrt(D)
    return base.astype(jnp.bfloat16)


def shard_levels(key, extent, cuts, least, high):
    factor_of, own = 1.0, jax.random.fold_in(key, 6)
    for dim, blocks in cuts:
        draws = jnp.exp(jax.random.uniform(jax.random.fold_in(own, dim), (blocks,), jnp.float32, least / len(cuts), high / len(cuts)))
        factor_of = factor_of * jnp.repeat(draws, extent[dim] // blocks).reshape([-1 if axis == dim else 1 for axis in range(len(extent))])
    return factor_of


def scatter_about(own_key, dims, scale, bound, shards=(), kind=jnp.bfloat16):
    loudness = shard_levels(own_key, dims, shards, -0.22, 0.18) if shards else 1.0
    values = jax.random.normal(own_key, dims, jnp.float32) * scale * loudness
    return jnp.minimum(jnp.maximum(values, -bound), bound).astype(kind)


def setup_inputs(seed: int = 0) -> dict:
    arg_keys = jax.random.split(jax.random.key(seed), 14)
    return {
        "vis_feat": draw_vis_feat(jax.random.fold_in(arg_keys[13], 71), 0),
        "ln_gain": jnp.clip(1.0 + 0.15 * jax.random.normal(arg_keys[1], (VF,), jnp.float32), 0.25, 1.75),
        "proj_weight": scatter_about(arg_keys[2], (VF, D), VF ** -0.5, 0.0546875, ((0, 4), (1, 8))),
        "text_embed": draw_text_embed(jax.random.fold_in(arg_keys[13], 71), 0),
        "rms_gain": jnp.clip(1.0 + 0.15 * jax.random.normal(arg_keys[4], (D,), jnp.float32), 0.25, 1.75),
        "wq": draw_wq(jax.random.fold_in(arg_keys[13], 71), 0),
        "wk": draw_wk(jax.random.fold_in(arg_keys[13], 71), 0),
        "wv": scatter_about(arg_keys[7], (D, KV * HEAD), D ** -0.5, 0.0625, ((0, 8), (1, 4))),
        "doc_ids": draw_doc_ids(jax.random.fold_in(arg_keys[13], 71), 0),
        "vis_slot": draw_vis_slot(jax.random.fold_in(arg_keys[13], 71), 0),
        "slot_token": draw_slot_token(jax.random.fold_in(arg_keys[13], 71), 0),
        "token_slot": draw_token_slot(jax.random.fold_in(arg_keys[13], 71), 0),
        "cotangent": scatter_about(arg_keys[12], (TOKENS, HEADS * HEAD), 1.0, 6.0, ((0, 8), (1, 4))),
    }


ln_eps = 1e-05
rms_eps = 1e-06
rope_base = 1000000.0
masked_score = -1e+30

def rope_tables(positions, head_width):
    half = head_width // 2
    frequency = rope_base ** (-(jnp.arange(half).astype(jnp.float32) * 2.0 / head_width))
    angle = positions.astype(jnp.float32)[:, None] * frequency[None, :]
    return (jnp.cos(angle), jnp.sin(angle))

def rotate(values, cosine, sine):
    half = values.shape[-1] // 2
    first = values[..., :half]
    second = values[..., half:]
    cos_rows = cosine[:, None, :]
    sin_rows = sine[:, None, :]
    return jnp.concatenate([first * cos_rows - second * sin_rows, second * cos_rows + first * sin_rows], axis=-1)

def unrotate(grads, cosine, sine):
    half = grads.shape[-1] // 2
    first = grads[..., :half]
    second = grads[..., half:]
    cos_rows = cosine[:, None, :]
    sin_rows = sine[:, None, :]
    return jnp.concatenate([first * cos_rows + second * sin_rows, second * cos_rows - first * sin_rows], axis=-1)

def norm_backward(rows, grads, gain):
    inv_rms = lax.rsqrt(lax.optimization_barrier(jnp.mean(rows * rows, axis=1, keepdims=True)) + rms_eps)
    scaled = grads * gain[None, :]
    inner = lax.optimization_barrier(jnp.mean(rows * scaled, axis=1, keepdims=True))
    return inv_rms * scaled - rows * (inv_rms * inv_rms * inv_rms) * inner

def attention_block(queries, keys, values, grads, allowed):
    scale = 1.0 / math.sqrt(queries.shape[-1])
    wide_q = queries.astype(jnp.float32)
    wide_k = keys.astype(jnp.float32)
    wide_v = values.astype(jnp.float32)
    wide_g = grads.astype(jnp.float32)
    scores = jnp.einsum('qhgd,khd->hgqk', wide_q, wide_k) * scale
    masked = jnp.where(allowed[None, None], scores, masked_score)
    peak = lax.optimization_barrier(jnp.max(masked, axis=-1, keepdims=True))
    raised = jnp.where(allowed[None, None], jnp.exp(masked - peak), 0.0)
    shares = raised / lax.optimization_barrier(jnp.sum(raised, axis=-1, keepdims=True))
    shares_low = shares.astype(jnp.bfloat16)
    wide_s = shares_low.astype(jnp.float32)
    context = jnp.einsum('hgqk,khd->qhgd', wide_s, wide_v).astype(jnp.bfloat16)
    share_grads = jnp.einsum('qhgd,khd->hgqk', wide_g, wide_v)
    delta = lax.optimization_barrier(jnp.sum(shares * share_grads, axis=-1, keepdims=True))
    score_grads = (shares * (share_grads - delta) * scale).astype(jnp.bfloat16).astype(jnp.float32)
    query_grads = jnp.einsum('hgqk,khd->qhgd', score_grads, wide_k)
    key_grads = jnp.einsum('hgqk,qhgd->khd', score_grads, wide_q)
    value_grads = jnp.einsum('hgqk,qhgd->khd', wide_s, wide_g)
    return (context, query_grads, key_grads, value_grads)

def reference(vis_feat, ln_gain, proj_weight, text_embed, rms_gain, wq, wk, wv, doc_ids, vis_slot, slot_token, token_slot, cotangent):
    features = vis_feat.astype(jnp.float32)
    row_mean = lax.optimization_barrier(jnp.sum(features, axis=1)) / VF
    row_var = lax.optimization_barrier(jnp.sum(features * features, axis=1)) / VF - row_mean * row_mean
    inv_std = lax.rsqrt(row_var + ln_eps)
    centred = (features - row_mean[:, None]) * inv_std[:, None]
    vis_normed = (centred * ln_gain[None, :]).astype(jnp.bfloat16)
    vis_embed = jnp.dot(vis_normed, proj_weight, preferred_element_type=jnp.float32).astype(jnp.bfloat16)
    positions = jnp.arange(TOKENS, dtype=jnp.int32)
    blocks = positions // TOK_DEV
    is_image = vis_slot >= 0
    slot_total = N_SEQ * CAPD
    global_slot = jnp.where(is_image, blocks * CAPD + vis_slot, slot_total).astype(jnp.int32)
    token_at = jnp.where(is_image, slot_token[jnp.minimum(global_slot, slot_total - 1)], 0).astype(jnp.int32)
    hidden = jnp.where(is_image[:, None], vis_embed[token_at], text_embed)
    hidden_wide = hidden.astype(jnp.float32)
    inv_rms = lax.rsqrt(lax.optimization_barrier(jnp.mean(hidden_wide * hidden_wide, axis=1, keepdims=True)) + rms_eps)
    normed = (hidden_wide * inv_rms * rms_gain[None, :]).astype(jnp.bfloat16)
    query_proj = jnp.dot(normed, wq, preferred_element_type=jnp.float32)
    key_proj = jnp.dot(normed, wk, preferred_element_type=jnp.float32)
    value_proj = jnp.dot(normed, wv, preferred_element_type=jnp.float32)
    cosine, sine = rope_tables(positions, HEAD)
    roped_queries = rotate(query_proj.reshape(TOKENS, HEADS, HEAD), cosine, sine).astype(jnp.bfloat16)
    roped_keys = rotate(key_proj.reshape(TOKENS, KV, HEAD), cosine, sine).astype(jnp.bfloat16)
    values = value_proj.astype(jnp.bfloat16).reshape(TOKENS, KV, HEAD)
    front = jnp.zeros((TOK_DEV, KV, HEAD), jnp.bfloat16)
    key_padded = jnp.concatenate([front, roped_keys], axis=0)
    value_padded = jnp.concatenate([front, values], axis=0)
    doc_marks = (doc_ids + 1).astype(jnp.int32)
    doc_padded = jnp.concatenate([jnp.zeros((TOK_DEV,), jnp.int32), doc_marks], axis=0)
    pos_padded = jnp.concatenate([positions[:TOK_DEV] - TOK_DEV, positions], axis=0)
    query_four = roped_queries.reshape(TOKENS, KV, GROUP, HEAD)
    grad_four = cotangent.reshape(TOKENS, KV, GROUP, HEAD)

    def one_block(index):
        start = (index * TOK_DEV).astype(jnp.int32)
        block_q = lax.dynamic_slice_in_dim(query_four, start, TOK_DEV, 0)
        block_g = lax.dynamic_slice_in_dim(grad_four, start, TOK_DEV, 0)
        block_k = lax.dynamic_slice_in_dim(key_padded, start, 2 * TOK_DEV, 0)
        block_v = lax.dynamic_slice_in_dim(value_padded, start, 2 * TOK_DEV, 0)
        query_docs = lax.dynamic_slice_in_dim(doc_marks, start, TOK_DEV, 0)
        key_docs = lax.dynamic_slice_in_dim(doc_padded, start, 2 * TOK_DEV, 0)
        query_pos = lax.dynamic_slice_in_dim(positions, start, TOK_DEV, 0)
        key_pos = lax.dynamic_slice_in_dim(pos_padded, start, 2 * TOK_DEV, 0)
        allowed = (key_docs[None, :] == query_docs[:, None]) & (key_pos[None, :] <= query_pos[:, None])
        return attention_block(block_q, block_k, block_v, block_g, allowed)
    context, query_grads, key_grads, value_grads = lax.map(one_block, jnp.arange(N_SEQ, dtype=jnp.int32))
    context = context.reshape(TOKENS, HEADS * HEAD)
    tail = jnp.zeros((1, TOK_DEV, KV, HEAD), jnp.float32)
    key_total = key_grads[:, TOK_DEV:] + jnp.concatenate([key_grads[1:, :TOK_DEV], tail], axis=0)
    value_total = value_grads[:, TOK_DEV:] + jnp.concatenate([value_grads[1:, :TOK_DEV], tail], axis=0)
    query_pre = unrotate(query_grads.reshape(TOKENS, HEADS, HEAD), cosine, sine).astype(jnp.bfloat16).reshape(TOKENS, HEADS * HEAD)
    key_pre = unrotate(key_total.reshape(TOKENS, KV, HEAD), cosine, sine).astype(jnp.bfloat16).reshape(TOKENS, KV * HEAD)
    value_pre = value_total.astype(jnp.bfloat16).reshape(TOKENS, KV * HEAD)
    slot_pos = jnp.zeros((slot_total,), jnp.int32).at[global_slot].set(positions, mode='drop')
    where_token = slot_pos[token_slot]
    norm_grads = jnp.dot(query_pre[where_token], wq.T, preferred_element_type=jnp.float32)
    norm_grads = norm_grads + jnp.dot(key_pre[where_token], wk.T, preferred_element_type=jnp.float32)
    norm_grads = norm_grads + jnp.dot(value_pre[where_token], wv.T, preferred_element_type=jnp.float32)
    embed_grads = norm_backward(vis_embed.astype(jnp.float32), norm_grads, rms_gain).astype(jnp.bfloat16)
    feature_grads = jnp.dot(embed_grads, proj_weight.T, preferred_element_type=jnp.float32)
    scaled = feature_grads * ln_gain[None, :]
    grad_mean = lax.optimization_barrier(jnp.sum(scaled, axis=1)) / VF
    grad_inner = lax.optimization_barrier(jnp.sum(scaled * centred, axis=1)) / VF
    vis_grad = (inv_std[:, None] * (scaled - grad_mean[:, None] - centred * grad_inner[:, None])).astype(jnp.bfloat16)
    return (context, vis_grad)
```

```python
import functools
import math

import jax
import jax.numpy as jnp
from jax import lax
from jax.experimental import pallas as pl
from jax.experimental.pallas import tpu as pltpu
from jax.sharding import PartitionSpec as P

VF = 12800
HEAD = 128
CAPD = 32
GROUP = 4


ln_eps = 1e-05
rms_eps = 1e-06
rope_base = 1000000.0
masked_score = -1e30


def shifted(x, axis, by):
    peers = lax.axis_size(axis)
    pairs = [(i, i + by) for i in range(peers) if 0 <= i + by < peers]
    return lax.ppermute(x, axis, pairs)


MESH = pl.DeviceIdType.MESH
VMEM_LIMIT = 56 * 1024 * 1024
NT = (((1,), (1,)), ((), ()))
TN = (((0,), (0,)), ((), ()))
NN = (((1,), (0,)), ((), ()))


def mul(a, b, dims=NN):
    return lax.dot_general(a, b, dims, preferred_element_type=jnp.float32)


def rope_rows(positions):
    half = HEAD // 2
    frequency = rope_base ** (-(jnp.arange(half).astype(jnp.float32) * 2.0 / HEAD))
    angle = positions.astype(jnp.float32)[:, None] * frequency[None, :]
    cosine, sine = jnp.cos(angle), jnp.sin(angle)
    return (
        jnp.concatenate([cosine, cosine], axis=1),
        jnp.concatenate([-sine, sine], axis=1),
    )


def attention_kernel(
    heads, proj_ref, own_ref, prev_ref, cot_ref, qdoc_ref, odoc_ref, pdoc_ref, cos_ref, sin_ref,
    ctx_ref, qg_ref, og_ref, pg_ref, kacc, vacc,
):
    rows = cos_ref.shape[0]
    groups = heads // GROUP
    tail = rows - CAPD
    edge = rows - HEAD
    scale = 1.0 / math.sqrt(HEAD)
    qdoc = qdoc_ref[...]
    near = qdoc == odoc_ref[...]
    row_at = lax.broadcasted_iota(jnp.int32, (rows, rows), 0)
    col_at = lax.broadcasted_iota(jnp.int32, (rows, rows), 1)
    mask1 = near & (col_at <= row_at)
    mask0 = qdoc == pdoc_ref[...]
    for group in range(groups):
        kc = slice(group * HEAD, (group + 1) * HEAD)
        vc = slice((groups + group) * HEAD, (groups + group + 1) * HEAD)
        kp, ko = prev_ref[:, kc], own_ref[:, kc]
        vp, vo = prev_ref[:, vc], own_ref[:, vc]
        kacc[...] = jnp.zeros_like(kacc)
        vacc[...] = jnp.zeros_like(vacc)

        def one_head(member, carry):
            at = pl.multiple_of((group * GROUP + member) * HEAD, HEAD)
            cols = pl.ds(at, HEAD)
            wide = proj_ref[:, cols]
            q = (wide * cos_ref[...] + pltpu.roll(wide, HEAD // 2, 1) * sin_ref[...]).astype(
                jnp.bfloat16
            )
            g = cot_ref[:, cols]
            s0 = jnp.where(mask0, mul(q, kp, NT) * scale, masked_score)
            s1 = jnp.where(mask1, mul(q, ko, NT) * scale, masked_score)
            peak = jnp.maximum(
                jnp.max(s0, axis=1, keepdims=True), jnp.max(s1, axis=1, keepdims=True)
            )
            e0 = jnp.where(mask0, jnp.exp(s0 - peak), 0.0)
            e1 = jnp.where(mask1, jnp.exp(s1 - peak), 0.0)
            total = jnp.sum(e0, axis=1, keepdims=True) + jnp.sum(e1, axis=1, keepdims=True)
            inverse = 1.0 / total
            p0, p1 = e0 * inverse, e1 * inverse
            l0, l1 = p0.astype(jnp.bfloat16), p1.astype(jnp.bfloat16)
            ctx_ref[:, cols] = (mul(l0, vp) + mul(l1, vo)).astype(jnp.bfloat16)
            d0, d1 = mul(g, vp, NT), mul(g, vo, NT)
            delta = jnp.sum(p0 * d0, axis=1, keepdims=True) + jnp.sum(
                p1 * d1, axis=1, keepdims=True
            )
            z0 = (p0 * (d0 - delta) * scale).astype(jnp.bfloat16)
            z1 = (p1 * (d1 - delta) * scale).astype(jnp.bfloat16)
            qg_ref[:, cols] = mul(z0[tail:], kp) + mul(z1[tail:], ko)
            kacc[0] += mul(z0[:, edge:], q, TN)
            kacc[1] += mul(z1[:, edge:], q, TN)
            vacc[0] += mul(l0[:, edge:], g, TN)
            vacc[1] += mul(l1[:, edge:], g, TN)
            return carry

        lax.fori_loop(0, GROUP, one_head, 0)
        pg_ref[:, kc] = kacc[0, HEAD - CAPD :].astype(jnp.bfloat16)
        pg_ref[:, vc] = vacc[0, HEAD - CAPD :].astype(jnp.bfloat16)
        og_ref[:, kc] = kacc[1, HEAD - CAPD :]
        og_ref[:, vc] = vacc[1, HEAD - CAPD :]


def attention(projected, own, prev, cotangent, qdoc, odoc, pdoc, cosine, sine, heads):
    rows = own.shape[0]
    groups = heads // GROUP
    return pl.pallas_call(
        functools.partial(attention_kernel, heads),
        out_shape=(
            jax.ShapeDtypeStruct((rows, heads * HEAD), jnp.bfloat16),
            jax.ShapeDtypeStruct((CAPD, heads * HEAD), jnp.float32),
            jax.ShapeDtypeStruct((CAPD, 2 * groups * HEAD), jnp.float32),
            jax.ShapeDtypeStruct((CAPD, 2 * groups * HEAD), jnp.bfloat16),
        ),
        scratch_shapes=[
            pltpu.VMEM((2, HEAD, HEAD), jnp.float32),
            pltpu.VMEM((2, HEAD, HEAD), jnp.float32),
        ],
        compiler_params=pltpu.CompilerParams(vmem_limit_bytes=VMEM_LIMIT),
    )(projected, own, prev, cotangent, qdoc, odoc, pdoc, cosine, sine)


def exchange(axis, peers, me, source, target, send_sem, recv_sem):
    copies = []
    for step in range(1, peers):
        peer = lax.rem(me + step, peers)
        copies.append(
            pltpu.make_async_remote_copy(
                src_ref=source(peer),
                dst_ref=target(step),
                send_sem=send_sem.at[step - 1],
                recv_sem=recv_sem.at[step - 1],
                device_id={axis: peer},
                device_id_type=MESH,
            )
        )
        copies[-1].start()
    return copies


def both_sums(first, second, lane):
    return jnp.where(
        lane < HEAD // 2,
        jnp.sum(first, axis=1, keepdims=True),
        jnp.sum(second, axis=1, keepdims=True),
    )


def backward_kernel(
    seqs, tps, heads,
    qg_ref, og_ref, pg_ref, cos_ref, sin_ref, pick_ref, route_ref, emb_ref, gain_ref,
    cen_ref, lng_ref, istd_ref, w_hbm, proj_hbm,
    out_ref,
    w_ref, proj_ref, back, pre, gath, part, psend, precv, stat, srecv, eg, fsend, frecv, vstat,
    vrecv, local_sem, back_sem, g_send, g_recv, p_send, p_recv, s_send, s_recv, e_send, e_recv,
    f_send, f_recv, v_send, v_recv,
):
    s, t = lax.axis_index("seq"), lax.axis_index("tp")
    groups = heads // GROUP
    vis = route_ref.shape[0]
    tok = vis // tps
    own_rows = vis // seqs
    width = w_ref.shape[0]
    feats = proj_ref.shape[0]
    load_w = pltpu.make_async_copy(w_hbm, w_ref, local_sem.at[0])
    load_proj = pltpu.make_async_copy(proj_hbm, proj_ref, local_sem.at[1])
    load_w.start()
    load_proj.start()

    barrier = pltpu.get_barrier_semaphore()
    for step in range(1, seqs):
        pl.semaphore_signal(
            barrier, inc=1, device_id={"seq": lax.rem(s + step, seqs)}, device_id_type=MESH
        )
    for step in range(1, tps):
        pl.semaphore_signal(
            barrier, inc=1, device_id={"tp": lax.rem(t + step, tps)}, device_id_type=MESH
        )
    pl.semaphore_wait(barrier, seqs - 1 + tps - 1)

    shift = pltpu.make_async_remote_copy(
        src_ref=pg_ref, dst_ref=back, send_sem=back_sem.at[0], recv_sem=back_sem.at[1],
        device_id={"seq": lax.rem(s + seqs - 1, seqs)}, device_id_type=MESH,
    )
    shift.start()
    cosine, sine = cos_ref[...], sin_ref[...]

    def unrotated(wide):
        return wide * cosine - pltpu.roll(wide, HEAD // 2, 1) * sine

    for head in range(heads):
        cols = slice(head * HEAD, (head + 1) * HEAD)
        pre[:, cols] = unrotated(qg_ref[:, cols]).astype(jnp.bfloat16)
    shift.wait()
    keep = jnp.where(s < seqs - 1, 1.0, 0.0)
    for group in range(2 * groups):
        cols = slice(group * HEAD, (group + 1) * HEAD)
        wide = og_ref[:, cols] + back[:, cols].astype(jnp.float32) * keep
        if group < groups:
            wide = unrotated(wide)
        pre[:, (heads + group) * HEAD : (heads + group + 1) * HEAD] = wide.astype(jnp.bfloat16)
    gath[0] = mul(pick_ref[...], pre[...]).astype(jnp.bfloat16)

    copies = exchange(
        "seq", seqs, s, lambda peer: gath.at[0], lambda step: gath.at[step], g_send, g_recv
    )
    load_w.wait()
    for copy in copies:
        copy.wait()
    slots = gath[...].reshape(seqs * CAPD, gath.shape[2])
    selected = mul(route_ref[...], slots).astype(jnp.bfloat16)
    part[...] = mul(selected, w_ref[...], NT)
    for step in range(1, tps):
        rows = pl.ds(pl.multiple_of(lax.rem(t + step, tps) * tok, 16), tok)
        psend[step - 1] = part[rows, :].astype(jnp.bfloat16)
    copies = []
    for step in range(1, tps):
        copies.append(
            pltpu.make_async_remote_copy(
                src_ref=psend.at[step - 1], dst_ref=precv.at[step - 1],
                send_sem=p_send.at[step - 1], recv_sem=p_recv.at[step - 1],
                device_id={"tp": lax.rem(t + step, tps)}, device_id_type=MESH,
            )
        )
        copies[-1].start()
    mine = pl.ds(pl.multiple_of(t * tok, 16), tok)
    norm_grads = part[mine, :]
    for step, copy in enumerate(copies):
        copy.wait()
        norm_grads += precv[step].astype(jnp.float32)
    emb = emb_ref[mine, :].astype(jnp.float32)
    scaled = norm_grads * gain_ref[...]
    lane = lax.broadcasted_iota(jnp.int32, (tok, HEAD), 1)
    stat[...] = both_sums(emb * emb, emb * scaled, lane)
    copies = exchange(
        "seq", seqs, s, lambda peer: stat, lambda step: srecv.at[step - 1], s_send, s_recv
    )
    sums = stat[...]
    for step, copy in enumerate(copies):
        copy.wait()
        sums += srecv[step]
    inv_rms = lax.rsqrt(sums[:, :1] / (width * seqs) + rms_eps)
    inner = sums[:, HEAD // 2 : HEAD // 2 + 1] / (width * seqs)
    eg[t] = (inv_rms * scaled - emb * (inv_rms * inv_rms * inv_rms) * inner).astype(jnp.bfloat16)
    copies = exchange("tp", tps, t, lambda peer: eg.at[t], lambda step: eg.at[t], e_send, e_recv)
    load_proj.wait()
    for copy in copies:
        copy.wait()
    grads = eg[...].reshape(vis, width)
    chunk = 5 * HEAD
    for begin in range(0, feats, chunk):
        cols = slice(begin, min(begin + chunk, feats))
        block = mul(grads, proj_ref[cols, :], NT)
        fsend[:, :, cols] = block.astype(jnp.bfloat16).reshape(seqs, own_rows, -1)
    copies = exchange(
        "seq", seqs, s, lambda peer: fsend.at[peer], lambda step: frecv.at[step - 1], f_send,
        f_recv,
    )
    total = fsend[s].astype(jnp.float32)
    for step, copy in enumerate(copies):
        copy.wait()
        total += frecv[step].astype(jnp.float32)
    centred = cen_ref[...]
    scaled = total * lng_ref[...]
    lane = lax.broadcasted_iota(jnp.int32, (own_rows, HEAD), 1)
    vstat[...] = both_sums(scaled, scaled * centred, lane)
    copies = exchange(
        "tp", tps, t, lambda peer: vstat, lambda step: vrecv.at[step - 1], v_send, v_recv
    )
    sums = vstat[...]
    for step, copy in enumerate(copies):
        copy.wait()
        sums += vrecv[step]
    mean = sums[:, :1] / VF
    inner = sums[:, HEAD // 2 : HEAD // 2 + 1] / VF
    out_ref[...] = (istd_ref[...] * (scaled - mean - centred * inner)).astype(jnp.bfloat16)


def backward(qg, og, pg, cosine, sine, pick, route, emb, gain, centred, lng, istd, w, proj, heads):
    seqs, tps = lax.axis_size("seq"), lax.axis_size("tp")
    vis = route.shape[0]
    tok, own_rows = vis // tps, vis // seqs
    width, cols = w.shape
    feats = proj.shape[0]
    bf, f32 = jnp.bfloat16, jnp.float32
    sem = pltpu.SemaphoreType.DMA
    vm = pl.BlockSpec(memory_space=pltpu.VMEM)
    hb = pl.BlockSpec(memory_space=pl.ANY)
    return pl.pallas_call(
        functools.partial(backward_kernel, seqs, tps, heads),
        out_shape=jax.ShapeDtypeStruct((own_rows, feats), bf),
        in_specs=[vm] * 12 + [hb] * 2,
        out_specs=vm,
        scratch_shapes=[
            pltpu.VMEM((width, cols), bf),
            pltpu.VMEM((feats, width), bf),
            pltpu.VMEM(pg.shape, bf),
            pltpu.VMEM((CAPD, cols), bf),
            pltpu.VMEM((seqs, CAPD, cols), bf),
            pltpu.VMEM((vis, width), f32),
            pltpu.VMEM((tps - 1, tok, width), bf),
            pltpu.VMEM((tps - 1, tok, width), bf),
            pltpu.VMEM((tok, HEAD), f32),
            pltpu.VMEM((seqs - 1, tok, HEAD), f32),
            pltpu.VMEM((tps, tok, width), bf),
            pltpu.VMEM((seqs, own_rows, feats), bf),
            pltpu.VMEM((seqs - 1, own_rows, feats), bf),
            pltpu.VMEM((own_rows, HEAD), f32),
            pltpu.VMEM((tps - 1, own_rows, HEAD), f32),
            sem((2,)),
            sem((2,)),
            sem((seqs - 1,)),
            sem((seqs - 1,)),
            sem((tps - 1,)),
            sem((tps - 1,)),
            sem((seqs - 1,)),
            sem((seqs - 1,)),
            sem((tps - 1,)),
            sem((tps - 1,)),
            sem((seqs - 1,)),
            sem((seqs - 1,)),
            sem((tps - 1,)),
            sem((tps - 1,)),
        ],
        compiler_params=pltpu.CompilerParams(
            collective_id=0, has_side_effects=True, vmem_limit_bytes=VMEM_LIMIT
        ),
    )(qg, og, pg, cosine, sine, pick, route, emb, gain, centred, lng, istd, w, proj)


def on_device(
    vis_feat,
    ln_gain,
    proj_weight,
    text_embed,
    rms_gain,
    wq,
    wk,
    wv,
    doc_ids,
    vis_slot,
    slot_token,
    token_slot,
    cotangent,
):
    seq_count = lax.axis_size("seq")
    my_index = lax.axis_index("seq")
    tok_rows = text_embed.shape[0]
    slot_cols = proj_weight.shape[1]
    features = vis_feat.astype(jnp.float32)
    row_total, row_squares = lax.psum(
        (jnp.sum(features, axis=1), jnp.sum(features * features, axis=1)), "tp"
    )
    row_mean = row_total / VF
    row_var = row_squares / VF - row_mean * row_mean
    inv_std = lax.rsqrt(row_var + ln_eps)
    centred = (features - row_mean[:, None]) * inv_std[:, None]
    vis_normed = (centred * ln_gain[None, :]).astype(jnp.bfloat16)
    partial_embed = jnp.dot(
        lax.all_gather(vis_normed, "seq", axis=0, tiled=True),
        proj_weight,
        preferred_element_type=jnp.float32,
    )
    slot_live = (slot_token >= 0)[:, None]
    slot_index = jnp.maximum(slot_token, 0)
    summed = lax.psum(partial_embed, "tp")
    embed = summed.astype(jnp.bfloat16)
    embed_rows = jnp.take(embed, slot_index, axis=0)
    outgoing = jnp.where(slot_live, embed_rows, jnp.zeros_like(embed_rows)).reshape(
        seq_count, CAPD, slot_cols
    )
    arrived = lax.all_to_all(outgoing, "seq", split_axis=0, concat_axis=2, tiled=True)[0]
    lanes = jnp.arange(CAPD, dtype=jnp.int32)
    one_hot = (vis_slot[:, None] == lanes[None, :]).astype(jnp.bfloat16)
    placed = jnp.dot(one_hot, arrived, preferred_element_type=jnp.float32).astype(jnp.bfloat16)
    is_image = vis_slot >= 0
    hidden = jnp.where(is_image[:, None], placed, text_embed)
    hidden_wide = hidden.astype(jnp.float32)
    inv_rms = lax.rsqrt(jnp.mean(hidden_wide * hidden_wide, axis=1, keepdims=True) + rms_eps)
    normed = (hidden_wide * inv_rms * rms_gain[None, :]).astype(jnp.bfloat16)
    stacked = jnp.concatenate([wq, wk, wv], axis=1)
    query_cols = wq.shape[1]
    key_cols = wk.shape[1]
    gathered = lax.all_gather(stacked, "seq", axis=0, tiled=True)
    projected = jnp.dot(normed, gathered, preferred_element_type=jnp.float32)
    heads = query_cols // HEAD
    groups = key_cols // HEAD
    positions = my_index * tok_rows + jnp.arange(tok_rows, dtype=jnp.int32)
    cosine, sine = rope_rows(positions)
    pieces = []
    for group in range(groups):
        wide = projected[:, query_cols + group * HEAD : query_cols + (group + 1) * HEAD]
        turned = jnp.concatenate([wide[:, HEAD // 2 :], wide[:, : HEAD // 2]], axis=1)
        pieces.append((wide * cosine + turned * sine).astype(jnp.bfloat16))
    pieces.append(projected[:, query_cols + key_cols :].astype(jnp.bfloat16))
    own = jnp.concatenate(pieces, axis=1)
    doc_marks = (doc_ids + 1).astype(jnp.bfloat16)
    prev_docs = shifted(doc_marks, "seq", 1)
    prev = shifted(own, "seq", 1)
    query_docs = doc_marks.astype(jnp.float32)
    context, query_grads, own_grads, prev_grads = attention(
        projected,
        own,
        prev,
        cotangent,
        query_docs[:, None],
        query_docs[None, :],
        prev_docs.astype(jnp.float32)[None, :],
        cosine,
        sine,
        heads,
    )
    tail = tok_rows - CAPD
    pick = (lanes[:, None] == vis_slot[None, tail:]).astype(jnp.bfloat16)
    slot_ids = jnp.arange(seq_count * CAPD, dtype=jnp.int32)
    source = (my_index - slot_ids // CAPD + seq_count) % seq_count
    held = source * CAPD + slot_ids % CAPD
    route = (token_slot[:, None] == held[None, :]).astype(jnp.bfloat16)
    gain = lax.dynamic_slice_in_dim(rms_gain, my_index * slot_cols, slot_cols, 0)
    vis_grad = backward(
        query_grads,
        own_grads,
        prev_grads,
        cosine[tail:],
        sine[tail:],
        pick,
        route,
        embed,
        gain[None, :],
        centred,
        ln_gain[None, :],
        inv_std[:, None],
        stacked,
        proj_weight,
        heads,
    )
    return (context, vis_grad)


def solution(mesh):
    return jax.shard_map(
        on_device,
        mesh=mesh,
        in_specs=(
            P("seq", "tp"),
            P("tp"),
            P("tp", "seq"),
            P("seq", None),
            P(),
            P("seq", "tp"),
            P("seq", "tp"),
            P("seq", "tp"),
            P("seq"),
            P("seq"),
            P(),
            P(),
            P("seq", "tp"),
        ),
        out_specs=(P("seq", "tp"), P("seq", "tp")),
        check_vma=False,
    )
```

```python
import functools
import math

import jax
import jax.numpy as jnp
from jax import lax
from jax.experimental import pallas as pl
from jax.experimental.pallas import tpu as pltpu
from jax.sharding import PartitionSpec as P

VF = 12800
HEAD = 128
CAPD = 32
GROUP = 4


ln_eps = 1e-05
rms_eps = 1e-06
rope_base = 1000000.0
masked_score = -1e30


def shifted(x, axis, by):
    peers = lax.axis_size(axis)
    pairs = [(i, i + by) for i in range(peers) if 0 <= i + by < peers]
    return lax.ppermute(x, axis, pairs)


MESH = pl.DeviceIdType.MESH
VMEM_LIMIT = 56 * 1024 * 1024
NT = (((1,), (1,)), ((), ()))
TN = (((0,), (0,)), ((), ()))
NN = (((1,), (0,)), ((), ()))


def mul(a, b, dims=NN):
    return lax.dot_general(a, b, dims, preferred_element_type=jnp.float32)


def rope_rows(positions):
    half = HEAD // 2
    frequency = rope_base ** (-(jnp.arange(half).astype(jnp.float32) * 2.0 / HEAD))
    angle = positions.astype(jnp.float32)[:, None] * frequency[None, :]
    cosine, sine = jnp.cos(angle), jnp.sin(angle)
    return (
        jnp.concatenate([cosine, cosine], axis=1),
        jnp.concatenate([-sine, sine], axis=1),
    )


def attention_kernel(
    heads, proj_ref, own_ref, prev_ref, cot_ref, qdoc_ref, odoc_ref, pdoc_ref, cos_ref, sin_ref,
    ctx_ref, qg_ref, og_ref, pg_ref, kacc, vacc,
):
    rows = cos_ref.shape[0]
    groups = heads // GROUP
    tail = rows - CAPD
    edge = rows - HEAD
    scale = 1.0 / math.sqrt(HEAD)
    qdoc = qdoc_ref[...]
    near = qdoc == odoc_ref[...]
    row_at = lax.broadcasted_iota(jnp.int32, (rows, rows), 0)
    col_at = lax.broadcasted_iota(jnp.int32, (rows, rows), 1)
    mask1 = near & (col_at <= row_at)
    mask0 = qdoc == pdoc_ref[...]
    for group in range(groups):
        kc = slice(group * HEAD, (group + 1) * HEAD)
        vc = slice((groups + group) * HEAD, (groups + group + 1) * HEAD)
        kp, ko = prev_ref[:, kc], own_ref[:, kc]
        vp, vo = prev_ref[:, vc], own_ref[:, vc]
        kacc[...] = jnp.zeros_like(kacc)
        vacc[...] = jnp.zeros_like(vacc)

        def one_head(member, carry):
            at = pl.multiple_of((group * GROUP + member) * HEAD, HEAD)
            cols = pl.ds(at, HEAD)
            wide = proj_ref[:, cols]
            q = (wide * cos_ref[...] + pltpu.roll(wide, HEAD // 2, 1) * sin_ref[...]).astype(
                jnp.bfloat16
            )
            g = cot_ref[:, cols]
            s0 = jnp.where(mask0, mul(q, kp, NT) * scale, masked_score)
            s1 = jnp.where(mask1, mul(q, ko, NT) * scale, masked_score)
            peak = jnp.maximum(
                jnp.max(s0, axis=1, keepdims=True), jnp.max(s1, axis=1, keepdims=True)
            )
            e0 = jnp.where(mask0, jnp.exp(s0 - peak), 0.0)
            e1 = jnp.where(mask1, jnp.exp(s1 - peak), 0.0)
            total = jnp.sum(e0, axis=1, keepdims=True) + jnp.sum(e1, axis=1, keepdims=True)
            inverse = 1.0 / total
            p0, p1 = e0 * inverse, e1 * inverse
            l0, l1 = p0.astype(jnp.bfloat16), p1.astype(jnp.bfloat16)
            ctx_ref[:, cols] = (mul(l0, vp) + mul(l1, vo)).astype(jnp.bfloat16)
            d0, d1 = mul(g, vp, NT), mul(g, vo, NT)
            delta = jnp.sum(p0 * d0, axis=1, keepdims=True) + jnp.sum(
                p1 * d1, axis=1, keepdims=True
            )
            z0 = (p0 * (d0 - delta) * scale).astype(jnp.bfloat16)
            z1 = (p1 * (d1 - delta) * scale).astype(jnp.bfloat16)
            qg_ref[:, cols] = mul(z0[tail:], kp) + mul(z1[tail:], ko)
            kacc[0] += mul(z0[:, edge:], q, TN)
            kacc[1] += mul(z1[:, edge:], q, TN)
            vacc[0] += mul(l0[:, edge:], g, TN)
            vacc[1] += mul(l1[:, edge:], g, TN)
            return carry

        lax.fori_loop(0, GROUP, one_head, 0)
        pg_ref[:, kc] = kacc[0, HEAD - CAPD :].astype(jnp.bfloat16)
        pg_ref[:, vc] = vacc[0, HEAD - CAPD :].astype(jnp.bfloat16)
        og_ref[:, kc] = kacc[1, HEAD - CAPD :]
        og_ref[:, vc] = vacc[1, HEAD - CAPD :]


def attention(projected, own, prev, cotangent, qdoc, odoc, pdoc, cosine, sine, heads):
    rows = own.shape[0]
    groups = heads // GROUP
    return pl.pallas_call(
        functools.partial(attention_kernel, heads),
        out_shape=(
            jax.ShapeDtypeStruct((rows, heads * HEAD), jnp.bfloat16),
            jax.ShapeDtypeStruct((CAPD, heads * HEAD), jnp.float32),
            jax.ShapeDtypeStruct((CAPD, 2 * groups * HEAD), jnp.float32),
            jax.ShapeDtypeStruct((CAPD, 2 * groups * HEAD), jnp.bfloat16),
        ),
        scratch_shapes=[
            pltpu.VMEM((2, HEAD, HEAD), jnp.float32),
            pltpu.VMEM((2, HEAD, HEAD), jnp.float32),
        ],
        compiler_params=pltpu.CompilerParams(vmem_limit_bytes=VMEM_LIMIT),
    )(projected, own, prev, cotangent, qdoc, odoc, pdoc, cosine, sine)


def exchange(axis, peers, me, source, target, send_sem, recv_sem):
    copies = []
    for step in range(1, peers):
        peer = lax.rem(me + step, peers)
        copies.append(
            pltpu.make_async_remote_copy(
                src_ref=source(peer),
                dst_ref=target(step),
                send_sem=send_sem.at[step - 1],
                recv_sem=recv_sem.at[step - 1],
                device_id={axis: peer},
                device_id_type=MESH,
            )
        )
        copies[-1].start()
    return copies


def both_sums(first, second, lane):
    return jnp.where(
        lane < HEAD // 2,
        jnp.sum(first, axis=1, keepdims=True),
        jnp.sum(second, axis=1, keepdims=True),
    )


def weight_loads(sources, target, sems):
    loads, at = [], 0
    for index, source in enumerate(sources):
        wide = source.shape[1]
        loads.append(
            pltpu.make_async_copy(source, target.at[:, at : at + wide], sems.at[index])
        )
        at += wide
    return loads


def greet(seqs, tps, s, t):
    barrier = pltpu.get_barrier_semaphore()
    for step in range(1, seqs):
        pl.semaphore_signal(
            barrier, inc=1, device_id={"seq": lax.rem(s + step, seqs)}, device_id_type=MESH
        )
    for step in range(1, tps):
        pl.semaphore_signal(
            barrier, inc=1, device_id={"tp": lax.rem(t + step, tps)}, device_id_type=MESH
        )
    pl.semaphore_wait(barrier, seqs - 1 + tps - 1)


def forward_kernel(
    seqs, tps, heads,
    feat_ref, lng_ref, route_ref, place_ref, image_ref, rgain_ref, cos_ref, sin_ref,
    wq_hbm, wk_hbm, wv_hbm, proj_hbm, text_hbm,
    query_ref, own_ref, prev_ref, emb_ref, cen_ref, istd_ref,
    gw, proj_ref, hid, acc, nrm, stat, vrecv, part, precv, emb_s, out_s, arr, kvs, kvr,
    local_sem, w_send, w_recv, v_send, v_recv, n_send, n_recv, p_send, p_recv, e_send, e_recv,
    a_send, a_recv, k_sem,
):
    s, t = lax.axis_index("seq"), lax.axis_index("tp")
    groups = heads // GROUP
    own_rows, feats = feat_ref.shape
    width = gw.shape[1]
    vis = own_rows * seqs
    tok = vis // tps
    rows = hid.shape[0]
    tail = rows - CAPD
    loads = weight_loads((wq_hbm, wk_hbm, wv_hbm), gw.at[s], local_sem)
    load_proj = pltpu.make_async_copy(proj_hbm, proj_ref, local_sem.at[3])
    load_text = pltpu.make_async_copy(text_hbm, hid, local_sem.at[4])
    for load in loads:
        load.start()
    load_proj.start()
    load_text.start()
    greet(seqs, tps, s, t)
    for load in loads:
        load.wait()

    def other(bits):
        low, mid, high = s % 2, (s // 2) % 2, s // 4
        low = 1 - low if bits & 1 else low
        mid = 1 - mid if bits & 2 else mid
        high = 1 - high if bits & 4 else high
        return high * 4 + mid * 2 + low

    half = width // 2
    parts = (pl.ds(0, half), pl.ds(half, half))

    def send(number, owner, piece, bits):
        where = gw.at[owner] if piece is None else gw.at[owner, parts[piece]]
        copy = pltpu.make_async_remote_copy(
            src_ref=where, dst_ref=where,
            send_sem=w_send.at[number], recv_sem=w_recv.at[number],
            device_id={"seq": other(bits)}, device_id_type=MESH,
        )
        copy.start()
        return copy

    grid = seqs == 8
    if grid:
        x_a = send(0, s, 0, 2)
        y_b = send(1, s, 1, 4)
        x_b = send(2, s, 1, 2)
        y_a = send(3, s, 0, 4)
        core = send(4, s, None, 1)
    else:
        spread = exchange(
            "seq", seqs, s, lambda peer: gw.at[s], lambda step: gw.at[s], w_send, w_recv
        )

    features = feat_ref[...].astype(jnp.float32)
    lane = lax.broadcasted_iota(jnp.int32, (own_rows, HEAD), 1)
    stat[...] = both_sums(features, features * features, lane)
    copies = exchange(
        "tp", tps, t, lambda peer: stat, lambda step: vrecv.at[step - 1], v_send, v_recv
    )
    sums = stat[...]
    for step, copy in enumerate(copies):
        copy.wait()
        sums += vrecv[step]
    mean = sums[:, :1] / VF
    var = sums[:, HEAD // 2 : HEAD // 2 + 1] / VF - mean * mean
    inv_std = lax.rsqrt(var + ln_eps)
    centred = (features - mean) * inv_std
    cen_ref[...] = centred
    istd_ref[...] = jnp.broadcast_to(inv_std, istd_ref.shape)
    nrm[s] = (centred * lng_ref[...]).astype(jnp.bfloat16)
    copies = exchange("seq", seqs, s, lambda peer: nrm.at[s], lambda step: nrm.at[s], n_send, n_recv)
    load_proj.wait()
    for copy in copies:
        copy.wait()
    part[...] = mul(nrm[...].reshape(vis, feats), proj_ref[...])
    copies = []
    for step in range(1, tps):
        peer = lax.rem(t + step, tps)
        copies.append(
            pltpu.make_async_remote_copy(
                src_ref=part.at[pl.ds(pl.multiple_of(peer * tok, 16), tok)],
                dst_ref=precv.at[step - 1],
                send_sem=p_send.at[step - 1], recv_sem=p_recv.at[step - 1],
                device_id={"tp": peer}, device_id_type=MESH,
            )
        )
        copies[-1].start()
    total = part[pl.ds(pl.multiple_of(t * tok, 16), tok), :]
    for step, copy in enumerate(copies):
        copy.wait()
        total += precv[step]
    emb_s[t] = total.astype(jnp.bfloat16)
    copies = exchange(
        "tp", tps, t, lambda peer: emb_s.at[t], lambda step: emb_s.at[t], e_send, e_recv
    )
    load_text.wait()
    for copy in copies:
        copy.wait()
    embed = emb_s[...].reshape(vis, width)
    emb_ref[...] = embed
    out_s[...] = mul(route_ref[...], embed).astype(jnp.bfloat16).reshape(seqs, CAPD, width)
    arr[s] = out_s[s]
    copies = exchange(
        "seq", seqs, s, lambda peer: out_s.at[peer], lambda step: arr.at[s], a_send, a_recv
    )
    if grid:
        x_a.wait()
        turn_y = send(5, other(2), 0, 4)
        y_b.wait()
        turn_x = send(6, other(4), 1, 2)
    for copy in copies:
        copy.wait()
    image = image_ref[...] > 0.0
    square = jnp.zeros((rows, 1), jnp.float32)
    for index in range(seqs):
        cols = slice(index * width, (index + 1) * width)
        placed = mul(place_ref[...], arr[index])
        text = hid[tail:, cols].astype(jnp.float32)
        hid[tail:, cols] = jnp.where(image, placed, text).astype(jnp.bfloat16)
        wide = hid[:, cols].astype(jnp.float32)
        square += jnp.sum(wide * wide, axis=1, keepdims=True)
    inv_rms = lax.rsqrt(square / (width * seqs) + rms_eps)

    def project(owner):
        cols = pl.ds(pl.multiple_of(owner * width, HEAD), width)
        wide = hid[:, cols].astype(jnp.float32)
        normed = (wide * inv_rms * rgain_ref[:, cols]).astype(jnp.bfloat16)
        return mul(normed, gw[owner])

    acc[...] = project(s)
    if grid:
        core.wait()
        x_b.wait()
        core_x = send(7, other(2), None, 1)
        y_a.wait()
        core_y = send(8, other(4), None, 1)
        acc[...] += project(other(1))
        acc[...] += project(other(2))
        acc[...] += project(other(4))
        core_x.wait()
        acc[...] += project(other(3))
        core_y.wait()
        acc[...] += project(other(5))
        turn_y.wait()
        core_a = send(9, other(6), 0, 1)
        turn_x.wait()
        core_b = send(10, other(6), 1, 1)
        acc[...] += project(other(6))
        core_a.wait()
        core_b.wait()
        acc[...] += project(other(7))
    else:
        for step, copy in enumerate(spread):
            copy.wait()
            acc[...] += project(lax.rem(s - step - 1 + seqs, seqs))
    key_at = heads * HEAD
    cosine, sine = cos_ref[...], sin_ref[...]
    for group in range(2 * groups):
        cols = slice(group * HEAD, (group + 1) * HEAD)
        wide = acc[:, key_at + group * HEAD : key_at + (group + 1) * HEAD]
        if group < groups:
            wide = wide * cosine + pltpu.roll(wide, HEAD // 2, 1) * sine
        kvs[:, cols] = wide.astype(jnp.bfloat16)
    shift = pltpu.make_async_remote_copy(
        src_ref=kvs, dst_ref=kvr, send_sem=k_sem.at[0], recv_sem=k_sem.at[1],
        device_id={"seq": lax.rem(s + 1, seqs)}, device_id_type=MESH,
    )
    shift.start()
    own_ref[...] = kvs[...]
    query_ref[...] = acc[:, :key_at]
    shift.wait()
    prev_ref[...] = kvr[...]


def forward(feat, lng, route, place, image, rgain, cosine, sine, weights, proj, text):
    seqs, tps = lax.axis_size("seq"), lax.axis_size("tp")
    own_rows, feats = feat.shape
    vis = own_rows * seqs
    tok = vis // tps
    rows = text.shape[0]
    width = weights[0].shape[0]
    query_cols = weights[0].shape[1]
    kv_cols = 2 * weights[1].shape[1]
    cols = query_cols + kv_cols
    heads = query_cols // HEAD
    bf, f32 = jnp.bfloat16, jnp.float32
    sem = pltpu.SemaphoreType.DMA
    vm = pl.BlockSpec(memory_space=pltpu.VMEM)
    hb = pl.BlockSpec(memory_space=pl.ANY)
    moves = 11 if seqs == 8 else seqs - 1
    return pl.pallas_call(
        functools.partial(forward_kernel, seqs, tps, heads),
        out_shape=(
            jax.ShapeDtypeStruct((rows, query_cols), f32),
            jax.ShapeDtypeStruct((rows, kv_cols), bf),
            jax.ShapeDtypeStruct((rows, kv_cols), bf),
            jax.ShapeDtypeStruct((vis, width), bf),
            jax.ShapeDtypeStruct((own_rows, feats), f32),
            jax.ShapeDtypeStruct((own_rows, HEAD), f32),
        ),
        in_specs=[vm] * 8 + [hb] * 5,
        out_specs=(vm,) * 6,
        scratch_shapes=[
            pltpu.VMEM((seqs, width, cols), bf),
            pltpu.VMEM((feats, width), bf),
            pltpu.VMEM(text.shape, bf),
            pltpu.VMEM((rows, cols), f32),
            pltpu.VMEM((seqs, own_rows, feats), bf),
            pltpu.VMEM((own_rows, HEAD), f32),
            pltpu.VMEM((tps - 1, own_rows, HEAD), f32),
            pltpu.VMEM((vis, width), f32),
            pltpu.VMEM((tps - 1, tok, width), f32),
            pltpu.VMEM((tps, tok, width), bf),
            pltpu.VMEM((seqs, CAPD, width), bf),
            pltpu.VMEM((seqs, CAPD, width), bf),
            pltpu.VMEM((rows, kv_cols), bf),
            pltpu.VMEM((rows, kv_cols), bf),
            sem((5,)),
            sem((moves,)),
            sem((moves,)),
            sem((tps - 1,)),
            sem((tps - 1,)),
            sem((seqs - 1,)),
            sem((seqs - 1,)),
            sem((tps - 1,)),
            sem((tps - 1,)),
            sem((tps - 1,)),
            sem((tps - 1,)),
            sem((seqs - 1,)),
            sem((seqs - 1,)),
            sem((2,)),
        ],
        compiler_params=pltpu.CompilerParams(
            collective_id=1, has_side_effects=True, vmem_limit_bytes=VMEM_LIMIT
        ),
    )(feat, lng, route, place, image, rgain, cosine, sine, *weights, proj, text)


def backward_kernel(
    seqs, tps, heads,
    qg_ref, og_ref, pg_ref, cos_ref, sin_ref, pick_ref, route_ref, emb_ref, gain_ref,
    cen_ref, lng_ref, istd_ref, wq_hbm, wk_hbm, wv_hbm, proj_hbm,
    out_ref,
    w_ref, proj_ref, back, pre, gath, part, psend, precv, stat, srecv, eg, fsend, frecv, vstat,
    vrecv, local_sem, back_sem, g_send, g_recv, p_send, p_recv, s_send, s_recv, e_send, e_recv,
    f_send, f_recv, v_send, v_recv,
):
    s, t = lax.axis_index("seq"), lax.axis_index("tp")
    groups = heads // GROUP
    vis = route_ref.shape[0]
    tok = vis // tps
    own_rows = vis // seqs
    width = w_ref.shape[0]
    feats = proj_ref.shape[0]
    load_w = weight_loads((wq_hbm, wk_hbm, wv_hbm), w_ref, local_sem)
    load_proj = pltpu.make_async_copy(proj_hbm, proj_ref, local_sem.at[3])
    for load in load_w:
        load.start()
    load_proj.start()

    greet(seqs, tps, s, t)
    shift = pltpu.make_async_remote_copy(
        src_ref=pg_ref, dst_ref=back, send_sem=back_sem.at[0], recv_sem=back_sem.at[1],
        device_id={"seq": lax.rem(s + seqs - 1, seqs)}, device_id_type=MESH,
    )
    shift.start()
    cosine, sine = cos_ref[...], sin_ref[...]

    def unrotated(wide):
        return wide * cosine - pltpu.roll(wide, HEAD // 2, 1) * sine

    for head in range(heads):
        cols = slice(head * HEAD, (head + 1) * HEAD)
        pre[:, cols] = unrotated(qg_ref[:, cols]).astype(jnp.bfloat16)
    shift.wait()
    keep = jnp.where(s < seqs - 1, 1.0, 0.0)
    for group in range(2 * groups):
        cols = slice(group * HEAD, (group + 1) * HEAD)
        wide = og_ref[:, cols] + back[:, cols].astype(jnp.float32) * keep
        if group < groups:
            wide = unrotated(wide)
        pre[:, (heads + group) * HEAD : (heads + group + 1) * HEAD] = wide.astype(jnp.bfloat16)
    gath[0] = mul(pick_ref[...], pre[...]).astype(jnp.bfloat16)

    copies = exchange(
        "seq", seqs, s, lambda peer: gath.at[0], lambda step: gath.at[step], g_send, g_recv
    )
    for load in load_w:
        load.wait()
    for copy in copies:
        copy.wait()
    slots = gath[...].reshape(seqs * CAPD, gath.shape[2])
    selected = mul(route_ref[...], slots).astype(jnp.bfloat16)
    part[...] = mul(selected, w_ref[...], NT)
    for step in range(1, tps):
        rows = pl.ds(pl.multiple_of(lax.rem(t + step, tps) * tok, 16), tok)
        psend[step - 1] = part[rows, :].astype(jnp.bfloat16)
    copies = []
    for step in range(1, tps):
        copies.append(
            pltpu.make_async_remote_copy(
                src_ref=psend.at[step - 1], dst_ref=precv.at[step - 1],
                send_sem=p_send.at[step - 1], recv_sem=p_recv.at[step - 1],
                device_id={"tp": lax.rem(t + step, tps)}, device_id_type=MESH,
            )
        )
        copies[-1].start()
    mine = pl.ds(pl.multiple_of(t * tok, 16), tok)
    norm_grads = part[mine, :]
    for step, copy in enumerate(copies):
        copy.wait()
        norm_grads += precv[step].astype(jnp.float32)
    emb = emb_ref[mine, :].astype(jnp.float32)
    scaled = norm_grads * gain_ref[...]
    lane = lax.broadcasted_iota(jnp.int32, (tok, HEAD), 1)
    stat[...] = both_sums(emb * emb, emb * scaled, lane)
    copies = exchange(
        "seq", seqs, s, lambda peer: stat, lambda step: srecv.at[step - 1], s_send, s_recv
    )
    sums = stat[...]
    for step, copy in enumerate(copies):
        copy.wait()
        sums += srecv[step]
    inv_rms = lax.rsqrt(sums[:, :1] / (width * seqs) + rms_eps)
    inner = sums[:, HEAD // 2 : HEAD // 2 + 1] / (width * seqs)
    eg[t] = (inv_rms * scaled - emb * (inv_rms * inv_rms * inv_rms) * inner).astype(jnp.bfloat16)
    copies = exchange("tp", tps, t, lambda peer: eg.at[t], lambda step: eg.at[t], e_send, e_recv)
    load_proj.wait()
    for copy in copies:
        copy.wait()
    grads = eg[...].reshape(vis, width)
    chunk = 5 * HEAD
    for begin in range(0, feats, chunk):
        cols = slice(begin, min(begin + chunk, feats))
        block = mul(grads, proj_ref[cols, :], NT)
        fsend[:, :, cols] = block.astype(jnp.bfloat16).reshape(seqs, own_rows, -1)
    copies = exchange(
        "seq", seqs, s, lambda peer: fsend.at[peer], lambda step: frecv.at[step - 1], f_send,
        f_recv,
    )
    total = fsend[s].astype(jnp.float32)
    for step, copy in enumerate(copies):
        copy.wait()
        total += frecv[step].astype(jnp.float32)
    centred = cen_ref[...]
    scaled = total * lng_ref[...]
    lane = lax.broadcasted_iota(jnp.int32, (own_rows, HEAD), 1)
    vstat[...] = both_sums(scaled, scaled * centred, lane)
    copies = exchange(
        "tp", tps, t, lambda peer: vstat, lambda step: vrecv.at[step - 1], v_send, v_recv
    )
    sums = vstat[...]
    for step, copy in enumerate(copies):
        copy.wait()
        sums += vrecv[step]
    mean = sums[:, :1] / VF
    inner = sums[:, HEAD // 2 : HEAD // 2 + 1] / VF
    out_ref[...] = (istd_ref[...] * (scaled - mean - centred * inner)).astype(jnp.bfloat16)


def backward(qg, og, pg, cosine, sine, pick, route, emb, gain, centred, lng, istd, weights, proj, heads):
    seqs, tps = lax.axis_size("seq"), lax.axis_size("tp")
    vis = route.shape[0]
    tok, own_rows = vis // tps, vis // seqs
    width = weights[0].shape[0]
    cols = sum(w.shape[1] for w in weights)
    feats = proj.shape[0]
    bf, f32 = jnp.bfloat16, jnp.float32
    sem = pltpu.SemaphoreType.DMA
    vm = pl.BlockSpec(memory_space=pltpu.VMEM)
    hb = pl.BlockSpec(memory_space=pl.ANY)
    return pl.pallas_call(
        functools.partial(backward_kernel, seqs, tps, heads),
        out_shape=jax.ShapeDtypeStruct((own_rows, feats), bf),
        in_specs=[vm] * 12 + [hb] * 4,
        out_specs=vm,
        scratch_shapes=[
            pltpu.VMEM((width, cols), bf),
            pltpu.VMEM((feats, width), bf),
            pltpu.VMEM(pg.shape, bf),
            pltpu.VMEM((CAPD, cols), bf),
            pltpu.VMEM((seqs, CAPD, cols), bf),
            pltpu.VMEM((vis, width), f32),
            pltpu.VMEM((tps - 1, tok, width), bf),
            pltpu.VMEM((tps - 1, tok, width), bf),
            pltpu.VMEM((tok, HEAD), f32),
            pltpu.VMEM((seqs - 1, tok, HEAD), f32),
            pltpu.VMEM((tps, tok, width), bf),
            pltpu.VMEM((seqs, own_rows, feats), bf),
            pltpu.VMEM((seqs - 1, own_rows, feats), bf),
            pltpu.VMEM((own_rows, HEAD), f32),
            pltpu.VMEM((tps - 1, own_rows, HEAD), f32),
            sem((4,)),
            sem((2,)),
            sem((seqs - 1,)),
            sem((seqs - 1,)),
            sem((tps - 1,)),
            sem((tps - 1,)),
            sem((seqs - 1,)),
            sem((seqs - 1,)),
            sem((tps - 1,)),
            sem((tps - 1,)),
            sem((seqs - 1,)),
            sem((seqs - 1,)),
            sem((tps - 1,)),
            sem((tps - 1,)),
        ],
        compiler_params=pltpu.CompilerParams(
            collective_id=0, has_side_effects=True, vmem_limit_bytes=VMEM_LIMIT
        ),
    )(qg, og, pg, cosine, sine, pick, route, emb, gain, centred, lng, istd, *weights, proj)


def on_device(
    vis_feat,
    ln_gain,
    proj_weight,
    text_embed,
    rms_gain,
    wq,
    wk,
    wv,
    doc_ids,
    vis_slot,
    slot_token,
    token_slot,
    cotangent,
):
    seq_count = lax.axis_size("seq")
    my_index = lax.axis_index("seq")
    tok_rows = text_embed.shape[0]
    slot_cols = proj_weight.shape[1]
    query_cols = wq.shape[1]
    heads = query_cols // HEAD
    positions = my_index * tok_rows + jnp.arange(tok_rows, dtype=jnp.int32)
    cosine, sine = rope_rows(positions)
    tail = tok_rows - CAPD
    lanes = jnp.arange(CAPD, dtype=jnp.int32)
    pick = (lanes[:, None] == vis_slot[None, tail:]).astype(jnp.bfloat16)
    place = (vis_slot[tail:, None] == lanes[None, :]).astype(jnp.bfloat16)
    image = (vis_slot[tail:, None] >= 0).astype(jnp.float32)
    tokens = jnp.arange(token_slot.shape[0], dtype=jnp.int32)
    out_route = (slot_token[:, None] == tokens[None, :]).astype(jnp.bfloat16)
    doc_marks = (doc_ids + 1).astype(jnp.bfloat16)
    prev_docs = shifted(doc_marks, "seq", 1)
    projected, own, prev, embed, centred, inv_std = forward(
        vis_feat,
        ln_gain[None, :],
        out_route,
        place,
        image,
        rms_gain[None, :],
        cosine,
        sine,
        (wq, wk, wv),
        proj_weight,
        text_embed,
    )
    query_docs = doc_marks.astype(jnp.float32)
    context, query_grads, own_grads, prev_grads = attention(
        projected,
        own,
        prev,
        cotangent,
        query_docs[:, None],
        query_docs[None, :],
        prev_docs.astype(jnp.float32)[None, :],
        cosine,
        sine,
        heads,
    )
    slot_ids = jnp.arange(seq_count * CAPD, dtype=jnp.int32)
    source = (my_index - slot_ids // CAPD + seq_count) % seq_count
    held = source * CAPD + slot_ids % CAPD
    route = (token_slot[:, None] == held[None, :]).astype(jnp.bfloat16)
    gain = lax.dynamic_slice_in_dim(rms_gain, my_index * slot_cols, slot_cols, 0)
    vis_grad = backward(
        query_grads,
        own_grads,
        prev_grads,
        cosine[tail:],
        sine[tail:],
        pick,
        route,
        embed,
        gain[None, :],
        centred,
        ln_gain[None, :],
        inv_std[:, :1],
        (wq, wk, wv),
        proj_weight,
        heads,
    )
    return (context, vis_grad)


def solution(mesh):
    return jax.shard_map(
        on_device,
        mesh=mesh,
        in_specs=(
            P("seq", "tp"),
            P("tp"),
            P("tp", "seq"),
            P("seq", None),
            P(),
            P("seq", "tp"),
            P("seq", "tp"),
            P("seq", "tp"),
            P("seq"),
            P("seq"),
            P(),
            P(),
            P("seq", "tp"),
        ),
        out_specs=(P("seq", "tp"), P("seq", "tp")),
        check_vma=False,
    )
```

```python
import functools
import math

import jax
import jax.numpy as jnp
from jax import lax
from jax.experimental import pallas as pl
from jax.experimental.pallas import tpu as pltpu
from jax.sharding import PartitionSpec as P

VF = 12800
HEAD = 128
CAPD = 32
GROUP = 4


ln_eps = 1e-05
rms_eps = 1e-06
rope_base = 1000000.0
masked_score = -1e30


def shifted(x, axis, by):
    peers = lax.axis_size(axis)
    pairs = [(i, i + by) for i in range(peers) if 0 <= i + by < peers]
    return lax.ppermute(x, axis, pairs)


MESH = pl.DeviceIdType.MESH
VMEM_LIMIT = 56 * 1024 * 1024
NT = (((1,), (1,)), ((), ()))
TN = (((0,), (0,)), ((), ()))
NN = (((1,), (0,)), ((), ()))


def mul(a, b, dims=NN):
    return lax.dot_general(a, b, dims, preferred_element_type=jnp.float32)


def rope_rows(positions):
    half = HEAD // 2
    frequency = rope_base ** (-(jnp.arange(half).astype(jnp.float32) * 2.0 / HEAD))
    angle = positions.astype(jnp.float32)[:, None] * frequency[None, :]
    cosine, sine = jnp.cos(angle), jnp.sin(angle)
    return (
        jnp.concatenate([cosine, cosine], axis=1),
        jnp.concatenate([-sine, sine], axis=1),
    )


def attention_kernel(
    heads, proj_ref, own_ref, prev_ref, cot_ref, qdoc_ref, odoc_ref, pdoc_ref, cos_ref, sin_ref,
    ctx_ref, qg_ref, og_ref, pg_ref, kacc, vacc,
):
    rows = cos_ref.shape[0]
    groups = heads // GROUP
    tail = rows - CAPD
    edge = rows - HEAD
    scale = 1.0 / math.sqrt(HEAD)
    qdoc = qdoc_ref[...]
    near = qdoc == odoc_ref[...]
    row_at = lax.broadcasted_iota(jnp.int32, (rows, rows), 0)
    col_at = lax.broadcasted_iota(jnp.int32, (rows, rows), 1)
    mask1 = near & (col_at <= row_at)
    mask0 = qdoc == pdoc_ref[...]
    for group in range(groups):
        kc = slice(group * HEAD, (group + 1) * HEAD)
        vc = slice((groups + group) * HEAD, (groups + group + 1) * HEAD)
        kp, ko = prev_ref[:, kc], own_ref[:, kc]
        vp, vo = prev_ref[:, vc], own_ref[:, vc]
        kacc[...] = jnp.zeros_like(kacc)
        vacc[...] = jnp.zeros_like(vacc)

        def one_head(member, carry):
            at = pl.multiple_of((group * GROUP + member) * HEAD, HEAD)
            cols = pl.ds(at, HEAD)
            wide = proj_ref[:, cols]
            q = (wide * cos_ref[...] + pltpu.roll(wide, HEAD // 2, 1) * sin_ref[...]).astype(
                jnp.bfloat16
            )
            g = cot_ref[:, cols]
            s0 = jnp.where(mask0, mul(q, kp, NT) * scale, masked_score)
            s1 = jnp.where(mask1, mul(q, ko, NT) * scale, masked_score)
            peak = jnp.maximum(
                jnp.max(s0, axis=1, keepdims=True), jnp.max(s1, axis=1, keepdims=True)
            )
            e0 = jnp.where(mask0, jnp.exp(s0 - peak), 0.0)
            e1 = jnp.where(mask1, jnp.exp(s1 - peak), 0.0)
            total = jnp.sum(e0, axis=1, keepdims=True) + jnp.sum(e1, axis=1, keepdims=True)
            inverse = 1.0 / total
            p0, p1 = e0 * inverse, e1 * inverse
            l0, l1 = p0.astype(jnp.bfloat16), p1.astype(jnp.bfloat16)
            ctx_ref[:, cols] = (mul(l0, vp) + mul(l1, vo)).astype(jnp.bfloat16)
            d0, d1 = mul(g, vp, NT), mul(g, vo, NT)
            delta = jnp.sum(p0 * d0, axis=1, keepdims=True) + jnp.sum(
                p1 * d1, axis=1, keepdims=True
            )
            z0 = (p0 * (d0 - delta) * scale).astype(jnp.bfloat16)
            z1 = (p1 * (d1 - delta) * scale).astype(jnp.bfloat16)
            qg_ref[:, cols] = mul(z0[tail:], kp) + mul(z1[tail:], ko)
            kacc[0] += mul(z0[:, edge:], q, TN)
            kacc[1] += mul(z1[:, edge:], q, TN)
            vacc[0] += mul(l0[:, edge:], g, TN)
            vacc[1] += mul(l1[:, edge:], g, TN)
            return carry

        lax.fori_loop(0, GROUP, one_head, 0)
        pg_ref[:, kc] = kacc[0, HEAD - CAPD :].astype(jnp.bfloat16)
        pg_ref[:, vc] = vacc[0, HEAD - CAPD :].astype(jnp.bfloat16)
        og_ref[:, kc] = kacc[1, HEAD - CAPD :]
        og_ref[:, vc] = vacc[1, HEAD - CAPD :]


def attention(projected, own, prev, cotangent, qdoc, odoc, pdoc, cosine, sine, heads):
    rows = own.shape[0]
    groups = heads // GROUP
    return pl.pallas_call(
        functools.partial(attention_kernel, heads),
        out_shape=(
            jax.ShapeDtypeStruct((rows, heads * HEAD), jnp.bfloat16),
            jax.ShapeDtypeStruct((CAPD, heads * HEAD), jnp.float32),
            jax.ShapeDtypeStruct((CAPD, 2 * groups * HEAD), jnp.float32),
            jax.ShapeDtypeStruct((CAPD, 2 * groups * HEAD), jnp.bfloat16),
        ),
        scratch_shapes=[
            pltpu.VMEM((2, HEAD, HEAD), jnp.float32),
            pltpu.VMEM((2, HEAD, HEAD), jnp.float32),
        ],
        compiler_params=pltpu.CompilerParams(vmem_limit_bytes=VMEM_LIMIT),
    )(projected, own, prev, cotangent, qdoc, odoc, pdoc, cosine, sine)


def exchange(axis, peers, me, source, target, send_sem, recv_sem):
    copies = []
    for step in range(1, peers):
        peer = lax.rem(me + step, peers)
        copies.append(
            pltpu.make_async_remote_copy(
                src_ref=source(peer),
                dst_ref=target(step),
                send_sem=send_sem.at[step - 1],
                recv_sem=recv_sem.at[step - 1],
                device_id={axis: peer},
                device_id_type=MESH,
            )
        )
        copies[-1].start()
    return copies


def both_sums(first, second, lane):
    return jnp.where(
        lane < HEAD // 2,
        jnp.sum(first, axis=1, keepdims=True),
        jnp.sum(second, axis=1, keepdims=True),
    )


def weight_loads(sources, target, sems):
    loads, at = [], 0
    for index, source in enumerate(sources):
        wide = source.shape[1]
        loads.append(
            pltpu.make_async_copy(source, target.at[:, at : at + wide], sems.at[index])
        )
        at += wide
    return loads


def greet(seqs, tps, s, t):
    barrier = pltpu.get_barrier_semaphore()
    for step in range(1, seqs):
        pl.semaphore_signal(
            barrier, inc=1, device_id={"seq": lax.rem(s + step, seqs)}, device_id_type=MESH
        )
    for step in range(1, tps):
        pl.semaphore_signal(
            barrier, inc=1, device_id={"tp": lax.rem(t + step, tps)}, device_id_type=MESH
        )
    pl.semaphore_wait(barrier, seqs - 1 + tps - 1)


def forward_kernel(
    seqs, tps, heads,
    feat_ref, lng_ref, route_ref, pick_ref, rgain_ref, cos_ref, sin_ref,
    wq_hbm, wk_hbm, wv_hbm, proj_hbm, text_hbm,
    query_ref, own_ref, prev_ref, emb_ref, cen_ref, istd_ref,
    gw, proj_ref, hid, acc, nrm, stat, vrecv, part, precv, emb_s, out_s, arr, kvs, kvr,
    local_sem, w_send, w_recv, v_send, v_recv, n_send, n_recv, p_send, p_recv, e_send, e_recv,
    a_send, a_recv, k_sem,
):
    s, t = lax.axis_index("seq"), lax.axis_index("tp")
    groups = heads // GROUP
    own_rows, feats = feat_ref.shape
    width = gw.shape[1]
    vis = own_rows * seqs
    tok = vis // tps
    rows = hid.shape[0]
    tail = rows - CAPD
    loads = weight_loads((wq_hbm, wk_hbm, wv_hbm), gw.at[s], local_sem)
    load_proj = pltpu.make_async_copy(proj_hbm, proj_ref, local_sem.at[3])
    load_text = pltpu.make_async_copy(text_hbm, hid, local_sem.at[4])
    for load in loads:
        load.start()
    load_proj.start()
    load_text.start()
    greet(seqs, tps, s, t)

    def other(bits):
        low, mid, high = s % 2, (s // 2) % 2, s // 4
        low = 1 - low if bits & 1 else low
        mid = 1 - mid if bits & 2 else mid
        high = 1 - high if bits & 4 else high
        return high * 4 + mid * 2 + low

    half = width // 2
    parts = (pl.ds(0, half), pl.ds(half, half))

    def send(number, owner, piece, bits):
        where = gw.at[owner] if piece is None else gw.at[owner, parts[piece]]
        copy = pltpu.make_async_remote_copy(
            src_ref=where, dst_ref=where,
            send_sem=w_send.at[number], recv_sem=w_recv.at[number],
            device_id={"seq": other(bits)}, device_id_type=MESH,
        )
        copy.start()
        return copy

    grid = seqs == 8
    features = feat_ref[...].astype(jnp.float32)
    lane = lax.broadcasted_iota(jnp.int32, (own_rows, HEAD), 1)
    stat[...] = both_sums(features, features * features, lane)
    copies = exchange(
        "tp", tps, t, lambda peer: stat, lambda step: vrecv.at[step - 1], v_send, v_recv
    )
    sums = stat[...]
    for step, copy in enumerate(copies):
        copy.wait()
        sums += vrecv[step]
    mean = sums[:, :1] / VF
    var = sums[:, HEAD // 2 : HEAD // 2 + 1] / VF - mean * mean
    inv_std = lax.rsqrt(var + ln_eps)
    centred = (features - mean) * inv_std
    cen_ref[...] = centred
    istd_ref[...] = jnp.broadcast_to(inv_std, istd_ref.shape)
    nrm[s] = (centred * lng_ref[...]).astype(jnp.bfloat16)
    copies = exchange("seq", seqs, s, lambda peer: nrm.at[s], lambda step: nrm.at[s], n_send, n_recv)
    for load in loads:
        load.wait()
    if grid:
        x_a = send(0, s, 0, 2)
        y_b = send(1, s, 1, 4)
        core = send(4, s, None, 1)
    else:
        spread = exchange(
            "seq", seqs, s, lambda peer: gw.at[s], lambda step: gw.at[s], w_send, w_recv
        )
    load_proj.wait()
    for copy in copies:
        copy.wait()
    part[...] = mul(nrm[...].reshape(vis, feats), proj_ref[...])
    copies = []
    for step in range(1, tps):
        peer = lax.rem(t + step, tps)
        copies.append(
            pltpu.make_async_remote_copy(
                src_ref=part.at[pl.ds(pl.multiple_of(peer * tok, 16), tok)],
                dst_ref=precv.at[step - 1],
                send_sem=p_send.at[step - 1], recv_sem=p_recv.at[step - 1],
                device_id={"tp": peer}, device_id_type=MESH,
            )
        )
        copies[-1].start()
    total = part[pl.ds(pl.multiple_of(t * tok, 16), tok), :]
    for step, copy in enumerate(copies):
        copy.wait()
        total += precv[step]
    emb_s[t] = total.astype(jnp.bfloat16)
    copies = exchange(
        "tp", tps, t, lambda peer: emb_s.at[t], lambda step: emb_s.at[t], e_send, e_recv
    )
    load_text.wait()
    for copy in copies:
        copy.wait()
    embed = emb_s[...].reshape(vis, width)
    emb_ref[...] = embed
    out_s[...] = mul(route_ref[...], embed).astype(jnp.bfloat16).reshape(seqs, CAPD, width)
    arr[s] = out_s[s]
    copies = exchange(
        "seq", seqs, s, lambda peer: out_s.at[peer], lambda step: arr.at[s], a_send, a_recv
    )
    if grid:
        x_b = send(2, s, 1, 2)
        y_a = send(3, s, 0, 4)
        x_a.wait()
        turn_y = send(5, other(2), 0, 4)
        y_b.wait()
        turn_x = send(6, other(4), 1, 2)
    for copy in copies:
        copy.wait()
    pick = pick_ref[...]
    image = mul(pick, jnp.ones((CAPD, HEAD), jnp.bfloat16), TN)[:, :1] > 0.5
    square = jnp.zeros((rows, 1), jnp.float32)
    for index in range(seqs):
        cols = slice(index * width, (index + 1) * width)
        placed = mul(pick, arr[index], TN)
        text = hid[tail:, cols].astype(jnp.float32)
        hid[tail:, cols] = jnp.where(image, placed, text).astype(jnp.bfloat16)
        wide = hid[:, cols].astype(jnp.float32)
        square += jnp.sum(wide * wide, axis=1, keepdims=True)
    inv_rms = lax.rsqrt(square / (width * seqs) + rms_eps)

    def project(owner):
        cols = pl.ds(pl.multiple_of(owner * width, HEAD), width)
        wide = hid[:, cols].astype(jnp.float32)
        normed = (wide * inv_rms * rgain_ref[:, cols]).astype(jnp.bfloat16)
        return mul(normed, gw[owner])

    acc[...] = project(s)
    if grid:
        core.wait()
        x_b.wait()
        core_x = send(7, other(2), None, 1)
        y_a.wait()
        core_y = send(8, other(4), None, 1)
        acc[...] += project(other(1))
        acc[...] += project(other(2))
        acc[...] += project(other(4))
        core_x.wait()
        acc[...] += project(other(3))
        core_y.wait()
        acc[...] += project(other(5))
        turn_y.wait()
        core_a = send(9, other(6), 0, 1)
        turn_x.wait()
        core_b = send(10, other(6), 1, 1)
        acc[...] += project(other(6))
        core_a.wait()
        core_b.wait()
        acc[...] += project(other(7))
    else:
        for step, copy in enumerate(spread):
            copy.wait()
            acc[...] += project(lax.rem(s - step - 1 + seqs, seqs))
    key_at = heads * HEAD
    cosine, sine = cos_ref[...], sin_ref[...]
    for group in range(2 * groups):
        cols = slice(group * HEAD, (group + 1) * HEAD)
        wide = acc[:, key_at + group * HEAD : key_at + (group + 1) * HEAD]
        if group < groups:
            wide = wide * cosine + pltpu.roll(wide, HEAD // 2, 1) * sine
        kvs[:, cols] = wide.astype(jnp.bfloat16)
    shift = pltpu.make_async_remote_copy(
        src_ref=kvs, dst_ref=kvr, send_sem=k_sem.at[0], recv_sem=k_sem.at[1],
        device_id={"seq": lax.rem(s + 1, seqs)}, device_id_type=MESH,
    )
    shift.start()
    own_ref[...] = kvs[...]
    query_ref[...] = acc[:, :key_at]
    shift.wait()
    prev_ref[...] = kvr[...]


def forward(feat, lng, route, pick, rgain, cosine, sine, weights, proj, text):
    seqs, tps = lax.axis_size("seq"), lax.axis_size("tp")
    own_rows, feats = feat.shape
    vis = own_rows * seqs
    tok = vis // tps
    rows = text.shape[0]
    width = weights[0].shape[0]
    query_cols = weights[0].shape[1]
    kv_cols = 2 * weights[1].shape[1]
    cols = query_cols + kv_cols
    heads = query_cols // HEAD
    bf, f32 = jnp.bfloat16, jnp.float32
    sem = pltpu.SemaphoreType.DMA
    vm = pl.BlockSpec(memory_space=pltpu.VMEM)
    hb = pl.BlockSpec(memory_space=pl.ANY)
    moves = 11 if seqs == 8 else seqs - 1
    return pl.pallas_call(
        functools.partial(forward_kernel, seqs, tps, heads),
        out_shape=(
            jax.ShapeDtypeStruct((rows, query_cols), f32),
            jax.ShapeDtypeStruct((rows, kv_cols), bf),
            jax.ShapeDtypeStruct((rows, kv_cols), bf),
            jax.ShapeDtypeStruct((vis, width), bf),
            jax.ShapeDtypeStruct((own_rows, feats), f32),
            jax.ShapeDtypeStruct((own_rows, HEAD), f32),
        ),
        in_specs=[vm] * 7 + [hb] * 5,
        out_specs=(vm,) * 6,
        scratch_shapes=[
            pltpu.VMEM((seqs, width, cols), bf),
            pltpu.VMEM((feats, width), bf),
            pltpu.VMEM(text.shape, bf),
            pltpu.VMEM((rows, cols), f32),
            pltpu.VMEM((seqs, own_rows, feats), bf),
            pltpu.VMEM((own_rows, HEAD), f32),
            pltpu.VMEM((tps - 1, own_rows, HEAD), f32),
            pltpu.VMEM((vis, width), f32),
            pltpu.VMEM((tps - 1, tok, width), f32),
            pltpu.VMEM((tps, tok, width), bf),
            pltpu.VMEM((seqs, CAPD, width), bf),
            pltpu.VMEM((seqs, CAPD, width), bf),
            pltpu.VMEM((rows, kv_cols), bf),
            pltpu.VMEM((rows, kv_cols), bf),
            sem((5,)),
            sem((moves,)),
            sem((moves,)),
            sem((tps - 1,)),
            sem((tps - 1,)),
            sem((seqs - 1,)),
            sem((seqs - 1,)),
            sem((tps - 1,)),
            sem((tps - 1,)),
            sem((tps - 1,)),
            sem((tps - 1,)),
            sem((seqs - 1,)),
            sem((seqs - 1,)),
            sem((2,)),
        ],
        compiler_params=pltpu.CompilerParams(
            collective_id=1, has_side_effects=True, vmem_limit_bytes=VMEM_LIMIT
        ),
    )(feat, lng, route, pick, rgain, cosine, sine, *weights, proj, text)


def backward_kernel(
    seqs, tps, heads,
    qg_ref, og_ref, pg_ref, cos_ref, sin_ref, pick_ref, route_ref, emb_ref, gain_ref,
    cen_ref, lng_ref, istd_ref, wq_hbm, wk_hbm, wv_hbm, proj_hbm,
    out_ref,
    w_ref, proj_ref, back, pre, gath, part, psend, precv, stat, srecv, eg, fsend, frecv, vstat,
    vrecv, local_sem, back_sem, g_send, g_recv, p_send, p_recv, s_send, s_recv, e_send, e_recv,
    f_send, f_recv, v_send, v_recv,
):
    s, t = lax.axis_index("seq"), lax.axis_index("tp")
    groups = heads // GROUP
    vis = route_ref.shape[1]
    tok = vis // tps
    own_rows = vis // seqs
    width = w_ref.shape[0]
    feats = proj_ref.shape[0]
    load_w = weight_loads((wq_hbm, wk_hbm, wv_hbm), w_ref, local_sem)
    load_proj = pltpu.make_async_copy(proj_hbm, proj_ref, local_sem.at[3])
    for load in load_w:
        load.start()
    load_proj.start()

    greet(seqs, tps, s, t)
    shift = pltpu.make_async_remote_copy(
        src_ref=pg_ref, dst_ref=back, send_sem=back_sem.at[0], recv_sem=back_sem.at[1],
        device_id={"seq": lax.rem(s + seqs - 1, seqs)}, device_id_type=MESH,
    )
    shift.start()
    cosine, sine = cos_ref[...], sin_ref[...]

    def unrotated(wide):
        return wide * cosine - pltpu.roll(wide, HEAD // 2, 1) * sine

    for head in range(heads):
        cols = slice(head * HEAD, (head + 1) * HEAD)
        pre[:, cols] = unrotated(qg_ref[:, cols]).astype(jnp.bfloat16)
    shift.wait()
    keep = jnp.where(s < seqs - 1, 1.0, 0.0)
    for group in range(2 * groups):
        cols = slice(group * HEAD, (group + 1) * HEAD)
        wide = og_ref[:, cols] + back[:, cols].astype(jnp.float32) * keep
        if group < groups:
            wide = unrotated(wide)
        pre[:, (heads + group) * HEAD : (heads + group + 1) * HEAD] = wide.astype(jnp.bfloat16)
    gath[s] = mul(pick_ref[...], pre[...]).astype(jnp.bfloat16)

    copies = exchange(
        "seq", seqs, s, lambda peer: gath.at[s], lambda step: gath.at[s], g_send, g_recv
    )
    for load in load_w:
        load.wait()
    for copy in copies:
        copy.wait()
    slots = gath[...].reshape(seqs * CAPD, gath.shape[2])
    selected = mul(route_ref[...], slots, TN).astype(jnp.bfloat16)
    part[...] = mul(selected, w_ref[...], NT)
    for step in range(1, tps):
        rows = pl.ds(pl.multiple_of(lax.rem(t + step, tps) * tok, 16), tok)
        psend[step - 1] = part[rows, :].astype(jnp.bfloat16)
    copies = []
    for step in range(1, tps):
        copies.append(
            pltpu.make_async_remote_copy(
                src_ref=psend.at[step - 1], dst_ref=precv.at[step - 1],
                send_sem=p_send.at[step - 1], recv_sem=p_recv.at[step - 1],
                device_id={"tp": lax.rem(t + step, tps)}, device_id_type=MESH,
            )
        )
        copies[-1].start()
    mine = pl.ds(pl.multiple_of(t * tok, 16), tok)
    norm_grads = part[mine, :]
    for step, copy in enumerate(copies):
        copy.wait()
        norm_grads += precv[step].astype(jnp.float32)
    emb = emb_ref[mine, :].astype(jnp.float32)
    scaled = norm_grads * gain_ref[:, pl.ds(pl.multiple_of(s * width, HEAD), width)]
    lane = lax.broadcasted_iota(jnp.int32, (tok, HEAD), 1)
    stat[...] = both_sums(emb * emb, emb * scaled, lane)
    copies = exchange(
        "seq", seqs, s, lambda peer: stat, lambda step: srecv.at[step - 1], s_send, s_recv
    )
    sums = stat[...]
    for step, copy in enumerate(copies):
        copy.wait()
        sums += srecv[step]
    inv_rms = lax.rsqrt(sums[:, :1] / (width * seqs) + rms_eps)
    inner = sums[:, HEAD // 2 : HEAD // 2 + 1] / (width * seqs)
    eg[t] = (inv_rms * scaled - emb * (inv_rms * inv_rms * inv_rms) * inner).astype(jnp.bfloat16)
    copies = exchange("tp", tps, t, lambda peer: eg.at[t], lambda step: eg.at[t], e_send, e_recv)
    load_proj.wait()
    for copy in copies:
        copy.wait()
    grads = eg[...].reshape(vis, width)
    chunk = 5 * HEAD
    for begin in range(0, feats, chunk):
        cols = slice(begin, min(begin + chunk, feats))
        block = mul(grads, proj_ref[cols, :], NT)
        fsend[:, :, cols] = block.astype(jnp.bfloat16).reshape(seqs, own_rows, -1)
    copies = exchange(
        "seq", seqs, s, lambda peer: fsend.at[peer], lambda step: frecv.at[step - 1], f_send,
        f_recv,
    )
    total = fsend[s].astype(jnp.float32)
    for step, copy in enumerate(copies):
        copy.wait()
        total += frecv[step].astype(jnp.float32)
    centred = cen_ref[...]
    scaled = total * lng_ref[...]
    lane = lax.broadcasted_iota(jnp.int32, (own_rows, HEAD), 1)
    vstat[...] = both_sums(scaled, scaled * centred, lane)
    copies = exchange(
        "tp", tps, t, lambda peer: vstat, lambda step: vrecv.at[step - 1], v_send, v_recv
    )
    sums = vstat[...]
    for step, copy in enumerate(copies):
        copy.wait()
        sums += vrecv[step]
    mean = sums[:, :1] / VF
    inner = sums[:, HEAD // 2 : HEAD // 2 + 1] / VF
    out_ref[...] = (istd_ref[...] * (scaled - mean - centred * inner)).astype(jnp.bfloat16)


def backward(qg, og, pg, cosine, sine, pick, route, emb, gain, centred, lng, istd, weights, proj, heads):
    seqs, tps = lax.axis_size("seq"), lax.axis_size("tp")
    vis = route.shape[1]
    tok, own_rows = vis // tps, vis // seqs
    width = weights[0].shape[0]
    cols = sum(w.shape[1] for w in weights)
    feats = proj.shape[0]
    bf, f32 = jnp.bfloat16, jnp.float32
    sem = pltpu.SemaphoreType.DMA
    vm = pl.BlockSpec(memory_space=pltpu.VMEM)
    hb = pl.BlockSpec(memory_space=pl.ANY)
    return pl.pallas_call(
        functools.partial(backward_kernel, seqs, tps, heads),
        out_shape=jax.ShapeDtypeStruct((own_rows, feats), bf),
        in_specs=[vm] * 12 + [hb] * 4,
        out_specs=vm,
        scratch_shapes=[
            pltpu.VMEM((width, cols), bf),
            pltpu.VMEM((feats, width), bf),
            pltpu.VMEM(pg.shape, bf),
            pltpu.VMEM((CAPD, cols), bf),
            pltpu.VMEM((seqs, CAPD, cols), bf),
            pltpu.VMEM((vis, width), f32),
            pltpu.VMEM((tps - 1, tok, width), bf),
            pltpu.VMEM((tps - 1, tok, width), bf),
            pltpu.VMEM((tok, HEAD), f32),
            pltpu.VMEM((seqs - 1, tok, HEAD), f32),
            pltpu.VMEM((tps, tok, width), bf),
            pltpu.VMEM((seqs, own_rows, feats), bf),
            pltpu.VMEM((seqs - 1, own_rows, feats), bf),
            pltpu.VMEM((own_rows, HEAD), f32),
            pltpu.VMEM((tps - 1, own_rows, HEAD), f32),
            sem((4,)),
            sem((2,)),
            sem((seqs - 1,)),
            sem((seqs - 1,)),
            sem((tps - 1,)),
            sem((tps - 1,)),
            sem((seqs - 1,)),
            sem((seqs - 1,)),
            sem((tps - 1,)),
            sem((tps - 1,)),
            sem((seqs - 1,)),
            sem((seqs - 1,)),
            sem((tps - 1,)),
            sem((tps - 1,)),
        ],
        compiler_params=pltpu.CompilerParams(
            collective_id=0, has_side_effects=True, vmem_limit_bytes=VMEM_LIMIT
        ),
    )(qg, og, pg, cosine, sine, pick, route, emb, gain, centred, lng, istd, *weights, proj)


def on_device(
    vis_feat,
    ln_gain,
    proj_weight,
    text_embed,
    rms_gain,
    wq,
    wk,
    wv,
    doc_ids,
    vis_slot,
    slot_token,
    token_slot,
    cotangent,
):
    seq_count = lax.axis_size("seq")
    my_index = lax.axis_index("seq")
    tok_rows = text_embed.shape[0]
    slot_cols = proj_weight.shape[1]
    query_cols = wq.shape[1]
    heads = query_cols // HEAD
    positions = my_index * tok_rows + jnp.arange(tok_rows, dtype=jnp.int32)
    cosine, sine = rope_rows(positions)
    tail = tok_rows - CAPD
    lanes = jnp.arange(CAPD, dtype=jnp.int32)
    pick = (lanes[:, None] == vis_slot[None, tail:]).astype(jnp.bfloat16)
    tokens = jnp.arange(token_slot.shape[0], dtype=jnp.int32)
    out_route = (slot_token[:, None] == tokens[None, :]).astype(jnp.bfloat16)
    doc_marks = (doc_ids + 1).astype(jnp.bfloat16)
    prev_docs = shifted(doc_marks, "seq", 1)
    projected, own, prev, embed, centred, inv_std = forward(
        vis_feat,
        ln_gain[None, :],
        out_route,
        pick,
        rms_gain[None, :],
        cosine,
        sine,
        (wq, wk, wv),
        proj_weight,
        text_embed,
    )
    query_docs = doc_marks.astype(jnp.float32)
    context, query_grads, own_grads, prev_grads = attention(
        projected,
        own,
        prev,
        cotangent,
        query_docs[:, None],
        query_docs[None, :],
        prev_docs.astype(jnp.float32)[None, :],
        cosine,
        sine,
        heads,
    )
    vis_grad = backward(
        query_grads,
        own_grads,
        prev_grads,
        cosine[tail:],
        sine[tail:],
        pick,
        out_route,
        embed,
        rms_gain[None, :],
        centred,
        ln_gain[None, :],
        inv_std[:, :1],
        (wq, wk, wv),
        proj_weight,
        heads,
    )
    return (context, vis_grad)


def solution(mesh):
    return jax.shard_map(
        on_device,
        mesh=mesh,
        in_specs=(
            P("seq", "tp"),
            P("tp"),
            P("tp", "seq"),
            P("seq", None),
            P(),
            P("seq", "tp"),
            P("seq", "tp"),
            P("seq", "tp"),
            P("seq"),
            P("seq"),
            P(),
            P(),
            P("seq", "tp"),
        ),
        out_specs=(P("seq", "tp"), P("seq", "tp")),
        check_vma=False,
    )
```

```python
import functools
import math

import jax
import jax.numpy as jnp
from jax import lax
from jax.experimental import pallas as pl
from jax.experimental.pallas import tpu as pltpu
from jax.sharding import PartitionSpec as P

VF = 12800
HEAD = 128
CAPD = 32
GROUP = 4


ln_eps = 1e-05
rms_eps = 1e-06
rope_base = 1000000.0
masked_score = -1e30


def shifted(x, axis, by):
    peers = lax.axis_size(axis)
    pairs = [(i, i + by) for i in range(peers) if 0 <= i + by < peers]
    return lax.ppermute(x, axis, pairs)


MESH = pl.DeviceIdType.MESH
VMEM_LIMIT = 56 * 1024 * 1024
NT = (((1,), (1,)), ((), ()))
TN = (((0,), (0,)), ((), ()))
NN = (((1,), (0,)), ((), ()))


def mul(a, b, dims=NN):
    return lax.dot_general(a, b, dims, preferred_element_type=jnp.float32)


def rope_rows(positions):
    half = HEAD // 2
    frequency = rope_base ** (-(jnp.arange(half).astype(jnp.float32) * 2.0 / HEAD))
    angle = positions.astype(jnp.float32)[:, None] * frequency[None, :]
    cosine, sine = jnp.cos(angle), jnp.sin(angle)
    return (
        jnp.concatenate([cosine, cosine], axis=1),
        jnp.concatenate([-sine, sine], axis=1),
    )


def attention_kernel(
    heads, proj_ref, own_ref, prev_ref, cot_ref, qdoc_ref, odoc_ref, pdoc_ref, cos_ref, sin_ref,
    ctx_ref, qg_ref, og_ref, pg_ref, kacc, vacc,
):
    rows = cos_ref.shape[0]
    groups = heads // GROUP
    tail = rows - CAPD
    edge = rows - HEAD
    scale = 1.0 / math.sqrt(HEAD)
    qdoc = qdoc_ref[...]
    near = qdoc == odoc_ref[...]
    row_at = lax.broadcasted_iota(jnp.int32, (rows, rows), 0)
    col_at = lax.broadcasted_iota(jnp.int32, (rows, rows), 1)
    mask1 = near & (col_at <= row_at)
    mask0 = qdoc == pdoc_ref[...]
    for group in range(groups):
        kc = slice(group * HEAD, (group + 1) * HEAD)
        vc = slice((groups + group) * HEAD, (groups + group + 1) * HEAD)
        kp, ko = prev_ref[:, kc], own_ref[:, kc]
        vp, vo = prev_ref[:, vc], own_ref[:, vc]
        kacc[...] = jnp.zeros_like(kacc)
        vacc[...] = jnp.zeros_like(vacc)

        def one_head(member, carry):
            at = pl.multiple_of((group * GROUP + member) * HEAD, HEAD)
            cols = pl.ds(at, HEAD)
            wide = proj_ref[:, cols]
            q = (wide * cos_ref[...] + pltpu.roll(wide, HEAD // 2, 1) * sin_ref[...]).astype(
                jnp.bfloat16
            )
            g = cot_ref[:, cols]
            s0 = jnp.where(mask0, mul(q, kp, NT) * scale, masked_score)
            s1 = jnp.where(mask1, mul(q, ko, NT) * scale, masked_score)
            peak = jnp.maximum(
                jnp.max(s0, axis=1, keepdims=True), jnp.max(s1, axis=1, keepdims=True)
            )
            e0 = jnp.where(mask0, jnp.exp(s0 - peak), 0.0)
            e1 = jnp.where(mask1, jnp.exp(s1 - peak), 0.0)
            total = jnp.sum(e0, axis=1, keepdims=True) + jnp.sum(e1, axis=1, keepdims=True)
            inverse = 1.0 / total
            p0, p1 = e0 * inverse, e1 * inverse
            l0, l1 = p0.astype(jnp.bfloat16), p1.astype(jnp.bfloat16)
            ctx_ref[:, cols] = (mul(l0, vp) + mul(l1, vo)).astype(jnp.bfloat16)
            d0, d1 = mul(g, vp, NT), mul(g, vo, NT)
            delta = jnp.sum(p0 * d0, axis=1, keepdims=True) + jnp.sum(
                p1 * d1, axis=1, keepdims=True
            )
            z0 = (p0 * (d0 - delta) * scale).astype(jnp.bfloat16)
            z1 = (p1 * (d1 - delta) * scale).astype(jnp.bfloat16)
            qg_ref[:, cols] = mul(z0[tail:], kp) + mul(z1[tail:], ko)
            kacc[0] += mul(z0[:, edge:], q, TN)
            kacc[1] += mul(z1[:, edge:], q, TN)
            vacc[0] += mul(l0[:, edge:], g, TN)
            vacc[1] += mul(l1[:, edge:], g, TN)
            return carry

        lax.fori_loop(0, GROUP, one_head, 0)
        pg_ref[:, kc] = kacc[0, HEAD - CAPD :].astype(jnp.bfloat16)
        pg_ref[:, vc] = vacc[0, HEAD - CAPD :].astype(jnp.bfloat16)
        og_ref[:, kc] = kacc[1, HEAD - CAPD :]
        og_ref[:, vc] = vacc[1, HEAD - CAPD :]


def attention(projected, own, prev, cotangent, qdoc, odoc, pdoc, cosine, sine, heads):
    rows = own.shape[0]
    groups = heads // GROUP
    return pl.pallas_call(
        functools.partial(attention_kernel, heads),
        out_shape=(
            jax.ShapeDtypeStruct((rows, heads * HEAD), jnp.bfloat16),
            jax.ShapeDtypeStruct((CAPD, heads * HEAD), jnp.float32),
            jax.ShapeDtypeStruct((CAPD, 2 * groups * HEAD), jnp.float32),
            jax.ShapeDtypeStruct((CAPD, 2 * groups * HEAD), jnp.bfloat16),
        ),
        scratch_shapes=[
            pltpu.VMEM((2, HEAD, HEAD), jnp.float32),
            pltpu.VMEM((2, HEAD, HEAD), jnp.float32),
        ],
        compiler_params=pltpu.CompilerParams(vmem_limit_bytes=VMEM_LIMIT),
    )(projected, own, prev, cotangent, qdoc, odoc, pdoc, cosine, sine)


def exchange(axis, peers, me, source, target, send_sem, recv_sem):
    copies = []
    for step in range(1, peers):
        peer = lax.rem(me + step, peers)
        copies.append(
            pltpu.make_async_remote_copy(
                src_ref=source(peer),
                dst_ref=target(step),
                send_sem=send_sem.at[step - 1],
                recv_sem=recv_sem.at[step - 1],
                device_id={axis: peer},
                device_id_type=MESH,
            )
        )
        copies[-1].start()
    return copies


def both_sums(first, second, lane):
    return jnp.where(
        lane < HEAD // 2,
        jnp.sum(first, axis=1, keepdims=True),
        jnp.sum(second, axis=1, keepdims=True),
    )


def weight_loads(sources, target, sems):
    loads, at = [], 0
    for index, source in enumerate(sources):
        wide = source.shape[1]
        loads.append(
            pltpu.make_async_copy(source, target.at[:, at : at + wide], sems.at[index])
        )
        at += wide
    return loads


def greet(seqs, tps, s, t):
    barrier = pltpu.get_barrier_semaphore()
    for step in range(1, seqs):
        pl.semaphore_signal(
            barrier, inc=1, device_id={"seq": lax.rem(s + step, seqs)}, device_id_type=MESH
        )
    for step in range(1, tps):
        pl.semaphore_signal(
            barrier, inc=1, device_id={"tp": lax.rem(t + step, tps)}, device_id_type=MESH
        )
    pl.semaphore_wait(barrier, seqs - 1 + tps - 1)


def forward_kernel(
    seqs, tps, heads,
    feat_ref, lng_ref, route_ref, pick_ref, rgain_ref, cos_ref, sin_ref,
    wq_hbm, wk_hbm, wv_hbm, proj_hbm, text_hbm,
    query_ref, own_ref, prev_ref, emb_ref, cen_ref, istd_ref,
    gw, proj_ref, hid, acc, nrm, stat, vrecv, part, precv, emb_s, out_s, arr, kvs, kvr,
    local_sem, w_send, w_recv, v_send, v_recv, n_send, n_recv, p_send, p_recv, e_send, e_recv,
    a_send, a_recv, k_sem,
):
    s, t = lax.axis_index("seq"), lax.axis_index("tp")
    groups = heads // GROUP
    own_rows, feats = feat_ref.shape
    width = gw.shape[1]
    vis = own_rows * seqs
    tok = vis // tps
    rows = hid.shape[0]
    tail = rows - CAPD
    loads = weight_loads((wq_hbm, wk_hbm, wv_hbm), gw.at[s], local_sem)
    load_proj = pltpu.make_async_copy(proj_hbm, proj_ref, local_sem.at[3])
    load_text = pltpu.make_async_copy(text_hbm, hid, local_sem.at[4])
    for load in loads:
        load.start()
    load_proj.start()
    load_text.start()
    greet(seqs, tps, s, t)

    def other(bits):
        low, mid, high = s % 2, (s // 2) % 2, s // 4
        low = 1 - low if bits & 1 else low
        mid = 1 - mid if bits & 2 else mid
        high = 1 - high if bits & 4 else high
        return high * 4 + mid * 2 + low

    half = width // 2
    parts = (pl.ds(0, half), pl.ds(half, half))

    def send(number, owner, piece, bits):
        where = gw.at[owner] if piece is None else gw.at[owner, parts[piece]]
        copy = pltpu.make_async_remote_copy(
            src_ref=where, dst_ref=where,
            send_sem=w_send.at[number], recv_sem=w_recv.at[number],
            device_id={"seq": other(bits)}, device_id_type=MESH,
        )
        copy.start()
        return copy

    grid = seqs == 8
    features = feat_ref[...].astype(jnp.float32)
    lane = lax.broadcasted_iota(jnp.int32, (own_rows, HEAD), 1)
    stat[...] = both_sums(features, features * features, lane)
    copies = exchange(
        "tp", tps, t, lambda peer: stat, lambda step: vrecv.at[step - 1], v_send, v_recv
    )
    sums = stat[...]
    for step, copy in enumerate(copies):
        copy.wait()
        sums += vrecv[step]
    mean = sums[:, :1] / VF
    var = sums[:, HEAD // 2 : HEAD // 2 + 1] / VF - mean * mean
    inv_std = lax.rsqrt(var + ln_eps)
    centred = (features - mean) * inv_std
    cen_ref[...] = centred
    istd_ref[...] = jnp.broadcast_to(inv_std, istd_ref.shape)
    nrm[s] = (centred * lng_ref[...]).astype(jnp.bfloat16)
    copies = exchange("seq", seqs, s, lambda peer: nrm.at[s], lambda step: nrm.at[s], n_send, n_recv)
    for load in loads:
        load.wait()
    if grid:
        x_a = send(0, s, 0, 2)
        y_b = send(1, s, 1, 4)
        core = send(4, s, None, 1)
    else:
        spread = exchange(
            "seq", seqs, s, lambda peer: gw.at[s], lambda step: gw.at[s], w_send, w_recv
        )
    load_proj.wait()
    for copy in copies:
        copy.wait()
    if grid:
        x_b = send(2, s, 1, 2)
        y_a = send(3, s, 0, 4)
    part[...] = mul(nrm[...].reshape(vis, feats), proj_ref[...])
    copies = []
    for step in range(1, tps):
        peer = lax.rem(t + step, tps)
        copies.append(
            pltpu.make_async_remote_copy(
                src_ref=part.at[pl.ds(pl.multiple_of(peer * tok, 16), tok)],
                dst_ref=precv.at[step - 1],
                send_sem=p_send.at[step - 1], recv_sem=p_recv.at[step - 1],
                device_id={"tp": peer}, device_id_type=MESH,
            )
        )
        copies[-1].start()
    total = part[pl.ds(pl.multiple_of(t * tok, 16), tok), :]
    for step, copy in enumerate(copies):
        copy.wait()
        total += precv[step]
    emb_s[t] = total.astype(jnp.bfloat16)
    copies = exchange(
        "tp", tps, t, lambda peer: emb_s.at[t], lambda step: emb_s.at[t], e_send, e_recv
    )
    load_text.wait()
    for copy in copies:
        copy.wait()
    embed = emb_s[...].reshape(vis, width)
    emb_ref[...] = embed
    out_s[...] = mul(route_ref[...], embed).astype(jnp.bfloat16).reshape(seqs, CAPD, width)
    arr[s] = out_s[s]
    copies = exchange(
        "seq", seqs, s, lambda peer: out_s.at[peer], lambda step: arr.at[s], a_send, a_recv
    )
    if grid:
        x_a.wait()
        turn_y = send(5, other(2), 0, 4)
        y_b.wait()
        turn_x = send(6, other(4), 1, 2)
    for copy in copies:
        copy.wait()
    pick = pick_ref[...]
    image = mul(pick, jnp.ones((CAPD, HEAD), jnp.bfloat16), TN)[:, :1] > 0.5
    square = jnp.zeros((rows, 1), jnp.float32)
    for index in range(seqs):
        cols = slice(index * width, (index + 1) * width)
        placed = mul(pick, arr[index], TN)
        text = hid[tail:, cols].astype(jnp.float32)
        hid[tail:, cols] = jnp.where(image, placed, text).astype(jnp.bfloat16)
        wide = hid[:, cols].astype(jnp.float32)
        square += jnp.sum(wide * wide, axis=1, keepdims=True)
    inv_rms = lax.rsqrt(square / (width * seqs) + rms_eps)

    def project(owner):
        cols = pl.ds(pl.multiple_of(owner * width, HEAD), width)
        wide = hid[:, cols].astype(jnp.float32)
        normed = (wide * inv_rms * rgain_ref[:, cols]).astype(jnp.bfloat16)
        return mul(normed, gw[owner])

    acc[...] = project(s)
    if grid:
        core.wait()
        x_b.wait()
        core_x = send(7, other(2), None, 1)
        y_a.wait()
        core_y = send(8, other(4), None, 1)
        acc[...] += project(other(1))
        acc[...] += project(other(2))
        acc[...] += project(other(4))
        core_x.wait()
        acc[...] += project(other(3))
        core_y.wait()
        acc[...] += project(other(5))
        turn_y.wait()
        core_a = send(9, other(6), 0, 1)
        turn_x.wait()
        core_b = send(10, other(6), 1, 1)
        acc[...] += project(other(6))
        core_a.wait()
        core_b.wait()
        acc[...] += project(other(7))
    else:
        for step, copy in enumerate(spread):
            copy.wait()
            acc[...] += project(lax.rem(s - step - 1 + seqs, seqs))
    key_at = heads * HEAD
    cosine, sine = cos_ref[...], sin_ref[...]
    for group in range(2 * groups):
        cols = slice(group * HEAD, (group + 1) * HEAD)
        wide = acc[:, key_at + group * HEAD : key_at + (group + 1) * HEAD]
        if group < groups:
            wide = wide * cosine + pltpu.roll(wide, HEAD // 2, 1) * sine
        kvs[:, cols] = wide.astype(jnp.bfloat16)
    shift = pltpu.make_async_remote_copy(
        src_ref=kvs, dst_ref=kvr, send_sem=k_sem.at[0], recv_sem=k_sem.at[1],
        device_id={"seq": lax.rem(s + 1, seqs)}, device_id_type=MESH,
    )
    shift.start()
    own_ref[...] = kvs[...]
    query_ref[...] = acc[:, :key_at]
    shift.wait()
    prev_ref[...] = kvr[...]


def forward(feat, lng, route, pick, rgain, cosine, sine, weights, proj, text):
    seqs, tps = lax.axis_size("seq"), lax.axis_size("tp")
    own_rows, feats = feat.shape
    vis = own_rows * seqs
    tok = vis // tps
    rows = text.shape[0]
    width = weights[0].shape[0]
    query_cols = weights[0].shape[1]
    kv_cols = 2 * weights[1].shape[1]
    cols = query_cols + kv_cols
    heads = query_cols // HEAD
    bf, f32 = jnp.bfloat16, jnp.float32
    sem = pltpu.SemaphoreType.DMA
    vm = pl.BlockSpec(memory_space=pltpu.VMEM)
    hb = pl.BlockSpec(memory_space=pl.ANY)
    moves = 11 if seqs == 8 else seqs - 1
    return pl.pallas_call(
        functools.partial(forward_kernel, seqs, tps, heads),
        out_shape=(
            jax.ShapeDtypeStruct((rows, query_cols), f32),
            jax.ShapeDtypeStruct((rows, kv_cols), bf),
            jax.ShapeDtypeStruct((rows, kv_cols), bf),
            jax.ShapeDtypeStruct((vis, width), bf),
            jax.ShapeDtypeStruct((own_rows, feats), f32),
            jax.ShapeDtypeStruct((own_rows, HEAD), f32),
        ),
        in_specs=[vm] * 7 + [hb] * 5,
        out_specs=(vm,) * 6,
        scratch_shapes=[
            pltpu.VMEM((seqs, width, cols), bf),
            pltpu.VMEM((feats, width), bf),
            pltpu.VMEM(text.shape, bf),
            pltpu.VMEM((rows, cols), f32),
            pltpu.VMEM((seqs, own_rows, feats), bf),
            pltpu.VMEM((own_rows, HEAD), f32),
            pltpu.VMEM((tps - 1, own_rows, HEAD), f32),
            pltpu.VMEM((vis, width), f32),
            pltpu.VMEM((tps - 1, tok, width), f32),
            pltpu.VMEM((tps, tok, width), bf),
            pltpu.VMEM((seqs, CAPD, width), bf),
            pltpu.VMEM((seqs, CAPD, width), bf),
            pltpu.VMEM((rows, kv_cols), bf),
            pltpu.VMEM((rows, kv_cols), bf),
            sem((5,)),
            sem((moves,)),
            sem((moves,)),
            sem((tps - 1,)),
            sem((tps - 1,)),
            sem((seqs - 1,)),
            sem((seqs - 1,)),
            sem((tps - 1,)),
            sem((tps - 1,)),
            sem((tps - 1,)),
            sem((tps - 1,)),
            sem((seqs - 1,)),
            sem((seqs - 1,)),
            sem((2,)),
        ],
        compiler_params=pltpu.CompilerParams(
            collective_id=1, has_side_effects=True, vmem_limit_bytes=VMEM_LIMIT
        ),
    )(feat, lng, route, pick, rgain, cosine, sine, *weights, proj, text)


def backward_kernel(
    seqs, tps, heads,
    qg_ref, og_ref, pg_ref, cos_ref, sin_ref, pick_ref, route_ref, emb_ref, gain_ref,
    cen_ref, lng_ref, istd_ref, wq_hbm, wk_hbm, wv_hbm, proj_hbm,
    out_ref,
    w_ref, proj_ref, back, pre, gath, part, psend, precv, stat, srecv, eg, fsend, frecv, vstat,
    vrecv, local_sem, back_sem, g_send, g_recv, p_send, p_recv, s_send, s_recv, e_send, e_recv,
    f_send, f_recv, v_send, v_recv,
):
    s, t = lax.axis_index("seq"), lax.axis_index("tp")
    groups = heads // GROUP
    vis = route_ref.shape[1]
    tok = vis // tps
    own_rows = vis // seqs
    width = w_ref.shape[0]
    feats = proj_ref.shape[0]
    load_w = weight_loads((wq_hbm, wk_hbm, wv_hbm), w_ref, local_sem)
    load_proj = pltpu.make_async_copy(proj_hbm, proj_ref, local_sem.at[3])
    for load in load_w:
        load.start()
    load_proj.start()

    greet(seqs, tps, s, t)
    shift = pltpu.make_async_remote_copy(
        src_ref=pg_ref, dst_ref=back, send_sem=back_sem.at[0], recv_sem=back_sem.at[1],
        device_id={"seq": lax.rem(s + seqs - 1, seqs)}, device_id_type=MESH,
    )
    shift.start()
    cosine, sine = cos_ref[...], sin_ref[...]

    def unrotated(wide):
        return wide * cosine - pltpu.roll(wide, HEAD // 2, 1) * sine

    for head in range(heads):
        cols = slice(head * HEAD, (head + 1) * HEAD)
        pre[:, cols] = unrotated(qg_ref[:, cols]).astype(jnp.bfloat16)
    shift.wait()
    keep = jnp.where(s < seqs - 1, 1.0, 0.0)
    for group in range(2 * groups):
        cols = slice(group * HEAD, (group + 1) * HEAD)
        wide = og_ref[:, cols] + back[:, cols].astype(jnp.float32) * keep
        if group < groups:
            wide = unrotated(wide)
        pre[:, (heads + group) * HEAD : (heads + group + 1) * HEAD] = wide.astype(jnp.bfloat16)
    gath[s] = mul(pick_ref[...], pre[...]).astype(jnp.bfloat16)

    copies = exchange(
        "seq", seqs, s, lambda peer: gath.at[s], lambda step: gath.at[s], g_send, g_recv
    )
    for load in load_w:
        load.wait()
    for copy in copies:
        copy.wait()
    slots = gath[...].reshape(seqs * CAPD, gath.shape[2])
    selected = mul(route_ref[...], slots, TN).astype(jnp.bfloat16)
    part[...] = mul(selected, w_ref[...], NT)
    for step in range(1, tps):
        rows = pl.ds(pl.multiple_of(lax.rem(t + step, tps) * tok, 16), tok)
        psend[step - 1] = part[rows, :].astype(jnp.bfloat16)
    copies = []
    for step in range(1, tps):
        copies.append(
            pltpu.make_async_remote_copy(
                src_ref=psend.at[step - 1], dst_ref=precv.at[step - 1],
                send_sem=p_send.at[step - 1], recv_sem=p_recv.at[step - 1],
                device_id={"tp": lax.rem(t + step, tps)}, device_id_type=MESH,
            )
        )
        copies[-1].start()
    mine = pl.ds(pl.multiple_of(t * tok, 16), tok)
    norm_grads = part[mine, :]
    for step, copy in enumerate(copies):
        copy.wait()
        norm_grads += precv[step].astype(jnp.float32)
    emb = emb_ref[mine, :].astype(jnp.float32)
    scaled = norm_grads * gain_ref[:, pl.ds(pl.multiple_of(s * width, HEAD), width)]
    lane = lax.broadcasted_iota(jnp.int32, (tok, HEAD), 1)
    stat[...] = both_sums(emb * emb, emb * scaled, lane)
    copies = exchange(
        "seq", seqs, s, lambda peer: stat, lambda step: srecv.at[step - 1], s_send, s_recv
    )
    sums = stat[...]
    for step, copy in enumerate(copies):
        copy.wait()
        sums += srecv[step]
    inv_rms = lax.rsqrt(sums[:, :1] / (width * seqs) + rms_eps)
    inner = sums[:, HEAD // 2 : HEAD // 2 + 1] / (width * seqs)
    eg[t] = (inv_rms * scaled - emb * (inv_rms * inv_rms * inv_rms) * inner).astype(jnp.bfloat16)
    copies = exchange("tp", tps, t, lambda peer: eg.at[t], lambda step: eg.at[t], e_send, e_recv)
    load_proj.wait()
    for copy in copies:
        copy.wait()
    grads = eg[...].reshape(vis, width)
    chunk = 5 * HEAD
    for begin in range(0, feats, chunk):
        cols = slice(begin, min(begin + chunk, feats))
        block = mul(grads, proj_ref[cols, :], NT)
        fsend[:, :, cols] = block.astype(jnp.bfloat16).reshape(seqs, own_rows, -1)
    copies = exchange(
        "seq", seqs, s, lambda peer: fsend.at[peer], lambda step: frecv.at[step - 1], f_send,
        f_recv,
    )
    total = fsend[s].astype(jnp.float32)
    for step, copy in enumerate(copies):
        copy.wait()
        total += frecv[step].astype(jnp.float32)
    centred = cen_ref[...]
    scaled = total * lng_ref[...]
    lane = lax.broadcasted_iota(jnp.int32, (own_rows, HEAD), 1)
    vstat[...] = both_sums(scaled, scaled * centred, lane)
    copies = exchange(
        "tp", tps, t, lambda peer: vstat, lambda step: vrecv.at[step - 1], v_send, v_recv
    )
    sums = vstat[...]
    for step, copy in enumerate(copies):
        copy.wait()
        sums += vrecv[step]
    mean = sums[:, :1] / VF
    inner = sums[:, HEAD // 2 : HEAD // 2 + 1] / VF
    out_ref[...] = (istd_ref[...] * (scaled - mean - centred * inner)).astype(jnp.bfloat16)


def backward(qg, og, pg, cosine, sine, pick, route, emb, gain, centred, lng, istd, weights, proj, heads):
    seqs, tps = lax.axis_size("seq"), lax.axis_size("tp")
    vis = route.shape[1]
    tok, own_rows = vis // tps, vis // seqs
    width = weights[0].shape[0]
    cols = sum(w.shape[1] for w in weights)
    feats = proj.shape[0]
    bf, f32 = jnp.bfloat16, jnp.float32
    sem = pltpu.SemaphoreType.DMA
    vm = pl.BlockSpec(memory_space=pltpu.VMEM)
    hb = pl.BlockSpec(memory_space=pl.ANY)
    return pl.pallas_call(
        functools.partial(backward_kernel, seqs, tps, heads),
        out_shape=jax.ShapeDtypeStruct((own_rows, feats), bf),
        in_specs=[vm] * 12 + [hb] * 4,
        out_specs=vm,
        scratch_shapes=[
            pltpu.VMEM((width, cols), bf),
            pltpu.VMEM((feats, width), bf),
            pltpu.VMEM(pg.shape, bf),
            pltpu.VMEM((CAPD, cols), bf),
            pltpu.VMEM((seqs, CAPD, cols), bf),
            pltpu.VMEM((vis, width), f32),
            pltpu.VMEM((tps - 1, tok, width), bf),
            pltpu.VMEM((tps - 1, tok, width), bf),
            pltpu.VMEM((tok, HEAD), f32),
            pltpu.VMEM((seqs - 1, tok, HEAD), f32),
            pltpu.VMEM((tps, tok, width), bf),
            pltpu.VMEM((seqs, own_rows, feats), bf),
            pltpu.VMEM((seqs - 1, own_rows, feats), bf),
            pltpu.VMEM((own_rows, HEAD), f32),
            pltpu.VMEM((tps - 1, own_rows, HEAD), f32),
            sem((4,)),
            sem((2,)),
            sem((seqs - 1,)),
            sem((seqs - 1,)),
            sem((tps - 1,)),
            sem((tps - 1,)),
            sem((seqs - 1,)),
            sem((seqs - 1,)),
            sem((tps - 1,)),
            sem((tps - 1,)),
            sem((seqs - 1,)),
            sem((seqs - 1,)),
            sem((tps - 1,)),
            sem((tps - 1,)),
        ],
        compiler_params=pltpu.CompilerParams(
            collective_id=0, has_side_effects=True, vmem_limit_bytes=VMEM_LIMIT
        ),
    )(qg, og, pg, cosine, sine, pick, route, emb, gain, centred, lng, istd, *weights, proj)


def on_device(
    vis_feat,
    ln_gain,
    proj_weight,
    text_embed,
    rms_gain,
    wq,
    wk,
    wv,
    doc_ids,
    vis_slot,
    slot_token,
    token_slot,
    cotangent,
):
    seq_count = lax.axis_size("seq")
    my_index = lax.axis_index("seq")
    tok_rows = text_embed.shape[0]
    slot_cols = proj_weight.shape[1]
    query_cols = wq.shape[1]
    heads = query_cols // HEAD
    positions = my_index * tok_rows + jnp.arange(tok_rows, dtype=jnp.int32)
    cosine, sine = rope_rows(positions)
    tail = tok_rows - CAPD
    lanes = jnp.arange(CAPD, dtype=jnp.int32)
    pick = (lanes[:, None] == vis_slot[None, tail:]).astype(jnp.bfloat16)
    tokens = jnp.arange(token_slot.shape[0], dtype=jnp.int32)
    out_route = (slot_token[:, None] == tokens[None, :]).astype(jnp.bfloat16)
    doc_marks = (doc_ids + 1).astype(jnp.bfloat16)
    prev_docs = shifted(doc_marks, "seq", 1)
    projected, own, prev, embed, centred, inv_std = forward(
        vis_feat,
        ln_gain[None, :],
        out_route,
        pick,
        rms_gain[None, :],
        cosine,
        sine,
        (wq, wk, wv),
        proj_weight,
        text_embed,
    )
    query_docs = doc_marks.astype(jnp.float32)
    context, query_grads, own_grads, prev_grads = attention(
        projected,
        own,
        prev,
        cotangent,
        query_docs[:, None],
        query_docs[None, :],
        prev_docs.astype(jnp.float32)[None, :],
        cosine,
        sine,
        heads,
    )
    vis_grad = backward(
        query_grads,
        own_grads,
        prev_grads,
        cosine[tail:],
        sine[tail:],
        pick,
        out_route,
        embed,
        rms_gain[None, :],
        centred,
        ln_gain[None, :],
        inv_std[:, :1],
        (wq, wk, wv),
        proj_weight,
        heads,
    )
    return (context, vis_grad)


def solution(mesh):
    return jax.shard_map(
        on_device,
        mesh=mesh,
        in_specs=(
            P("seq", "tp"),
            P("tp"),
            P("tp", "seq"),
            P("seq", None),
            P(),
            P("seq", "tp"),
            P("seq", "tp"),
            P("seq", "tp"),
            P("seq"),
            P("seq"),
            P(),
            P(),
            P("seq", "tp"),
        ),
        out_specs=(P("seq", "tp"), P("seq", "tp")),
        check_vma=False,
    )
```
